128 devices in a mesh: dp: 4 (over z), fsdp: 32 (over y, x, core).
Axes of the slice: x: 4, y: 4, z: 4, core: 2. Of those that a mesh axis runs over, the one named last changes fastest.
Arguments:
- query_attn: bfloat16 [16384, 2048], P(('dp', 'fsdp')), may hold values from -6 to 6
- query_resid: bfloat16 [16384, 4096], P(('dp', 'fsdp')), may hold values from -6 to 6
- passage_attn: bfloat16 [49152, 2048], P(('dp', 'fsdp')), may hold values from -6 to 6
- passage_resid: bfloat16 [49152, 4096], P(('dp', 'fsdp')), may hold values from -6 to 6
- out_weight: bfloat16 [2048, 4096], P('fsdp'), may hold values from -0.125 to 0.125
- hard_lists: int32 [32, 4, 2], P('fsdp'), may hold values from 0 to 11, as said below
- positive: int32 [16384], P(('dp', 'fsdp')), may hold values from 0 to 383
Outputs:
- query_loss: float32 [16384], P(('dp', 'fsdp'))
- query_attn_grad: bfloat16 [16384, 2048], P(('dp', 'fsdp'))
- query_resid_grad: bfloat16 [16384, 4096], P(('dp', 'fsdp'))
- passage_attn_grad: bfloat16 [49152, 2048], P(('dp', 'fsdp'))
- passage_resid_grad: bfloat16 [49152, 4096], P(('dp', 'fsdp'))
- weight_grad: float32 [2048, 4096], P('fsdp')
The draws below stay inside these ranges and needn't reach their ends.
Inputs may be any that keep to these rules, and one draw needn't show every extreme that they name: For each fsdp index f and dp index d, the 2 entries of hard_lists[f, d] are p * 3 + b, naming block b of the device with dp index p and fsdp index f, for 2 different p all unlike d.
All inputs are finite; a program needn't handle non-finite values.
Results may differ from the reference program's by a relative error of at most 0.024.
Values may be sent and summed in bfloat16 or wider, within the bound.
No kernel may reach another device: no remote copies, remote signals or barrier semaphores. Data moves between devices by JAX's collectives and lax.ppermute only.
A program may use at most 128 MiB of HBM per device.

```python
import jax
import jax.numpy as jnp
from jax import lax

D = 4096
HD = 2048
BLOCK = 128
K = 2
NBLK = 3
QUERIES = 16384
PASSAGES = 49152
N_DP = 4
N_FSDP = 32


def common_rows(key, salt, breadth):
    return jax.random.normal(jax.random.fold_in(key, salt), (PASSAGES, breadth), jnp.float32)


def draw_query_attn(key, part):
    key = jax.random.fold_in(key, 2)
    fresh = jax.random.normal(key, (QUERIES, HD), jnp.float32)
    return jnp.clip(fresh, -6.0, 6.0).astype(jnp.bfloat16)


def draw_query_resid(key, part):
    key = jax.random.fold_in(key, 3)
    fresh = jax.random.normal(key, (QUERIES, D), jnp.float32)
    return jnp.clip(fresh, -6.0, 6.0).astype(jnp.bfloat16)


def draw_passage_attn(key, part):
    source = common_rows(key, 101, HD)
    return jnp.clip(source, -6.0, 6.0).astype(jnp.bfloat16)


def draw_passage_resid(key, part):
    source = common_rows(key, 102, D)
    return jnp.clip(source, -6.0, 6.0).astype(jnp.bfloat16)


def draw_hard_lists(key, part):
    key = jax.random.fold_in(key, 11)
    first_key, second_key, third_key = jax.random.split(key, 3)
    noise = jax.random.randint(first_key, (N_FSDP, N_DP, N_DP - 1), 0, 1 << 20) * N_DP
    noise = noise + jnp.arange(N_DP - 1, dtype=jnp.int32)[None, None, :]
    order = jnp.argsort(noise, axis=-1)[:, :, :K].astype(jnp.int32)
    peers = (jnp.arange(N_DP, dtype=jnp.int32)[None, :, None] + 1 + order) % N_DP
    first_block = jax.random.randint(second_key, (N_FSDP, N_DP, K), 0, NBLK)
    second_block = jax.random.randint(third_key, (N_FSDP, N_DP, K), 0, NBLK)
    chosen = jnp.minimum(first_block, second_block)
    return (peers * NBLK + chosen).astype(jnp.int32)


def plant(values, own_key, low, high):
    longest = values.shape.index(max(values.shape))
    spots = []
    for shift in (0, 1):
        where = [jax.random.randint(jax.random.fold_in(own_key, axis), (), 0, length) for axis, length in enumerate(values.shape)]
        where[longest] = (where[longest] + shift) % values.shape[longest]
        spots.append(tuple(where))
    return values.at[spots[0]].set(low).at[spots[1]].set(high)


def level_of(key, extent, shards, least, top_value):
    level = 1.0
    for axis_at, blocks in shards:
        heights = jax.random.uniform(jax.random.fold_in(jax.random.fold_in(key, 6), axis_at), (blocks,), jnp.float32, least / len(shards), top_value / len(shards))
        level = level * jnp.repeat(jnp.exp(heights), extent[axis_at] // blocks).reshape((-1,) + (1,) * (len(extent) - 1 - axis_at))
    return level


def gaussian(stream_key, shape, width, reach, pieces=(), held_as=jnp.bfloat16):
    array = jax.random.normal(stream_key, shape, jnp.float32) * width
    if len(pieces) > 0:
        array = level_of(stream_key, shape, pieces, -0.22, 0.18) * array
    return jnp.clip(array, min=-reach, max=reach).astype(held_as)


def setup_inputs(seed: int = 0) -> dict:
    key_of = jax.random.split(jax.random.key(seed), 8)
    query_attn = draw_query_attn(jax.random.fold_in(key_of[7], 71), 0)
    query_resid = draw_query_resid(jax.random.fold_in(key_of[7], 71), 0)
    passage_attn = draw_passage_attn(jax.random.fold_in(key_of[7], 71), 0)
    passage_resid = draw_passage_resid(jax.random.fold_in(key_of[7], 71), 0)
    out_weight = gaussian(key_of[4], (HD, D), HD ** -0.5, 0.125, ((0, 32),))
    hard_lists = draw_hard_lists(jax.random.fold_in(key_of[7], 71), 0)
    positive = plant(jax.random.randint(key_of[6], (QUERIES,), 0, NBLK * BLOCK), jax.random.fold_in(key_of[6], 1), 0, (NBLK * BLOCK) - 1).astype(jnp.int32)
    return {"query_attn": query_attn, "query_resid": query_resid, "passage_attn": passage_attn, "passage_resid": passage_resid, "out_weight": out_weight, "hard_lists": hard_lists, "positive": positive}


sharpness = 250.0
epsilon = 1e-06

def embed(attend, stream, weight):
    mixed = stream.astype(jnp.float32) + jnp.dot(attend, weight, preferred_element_type=jnp.float32)
    factor = lax.rsqrt(lax.optimization_barrier(jnp.sum(mixed * mixed, axis=-1, keepdims=True)) + epsilon)
    return (mixed * factor, factor)

def unembed(upstream, unit_rows, factor):
    inner = lax.optimization_barrier(jnp.sum(unit_rows * upstream, axis=-1, keepdims=True))
    return ((upstream - unit_rows * inner) * factor).astype(jnp.bfloat16)

def reference(query_attn, query_resid, passage_attn, passage_resid, out_weight, hard_lists, positive):
    query_unit, query_factor = embed(query_attn, query_resid, out_weight)
    passage_unit, passage_factor = embed(passage_attn, passage_resid, out_weight)
    query_low = query_unit.astype(jnp.bfloat16)
    passage_low = passage_unit.astype(jnp.bfloat16)
    pass_rows = NBLK * BLOCK
    devices = N_DP * N_FSDP

    def one_device(device):
        dp_index = device // N_FSDP
        fsdp_index = device % N_FSDP
        queries = lax.dynamic_slice_in_dim(query_low, device * BLOCK, BLOCK, 0)
        nearby = lax.dynamic_slice_in_dim(passage_low, device * pass_rows, pass_rows, 0)
        entries = hard_lists[fsdp_index, dp_index]
        owners = entries // NBLK * N_FSDP + fsdp_index
        starts = (owners * pass_rows + entries % NBLK * BLOCK).astype(jnp.int32)
        remote = [lax.dynamic_slice_in_dim(passage_low, starts[member], BLOCK, 0) for member in range(K)]
        candidates = jnp.concatenate([nearby] + remote, axis=0)
        scores = sharpness * jnp.dot(queries, candidates.T, preferred_element_type=jnp.float32)
        highest = lax.optimization_barrier(jnp.max(scores, axis=1, keepdims=True))
        log_total = highest + jnp.log(lax.optimization_barrier(jnp.sum(jnp.exp(scores - highest), axis=1, keepdims=True)))
        targets = lax.dynamic_slice_in_dim(positive, device * BLOCK, BLOCK, 0)
        onehot = (jnp.arange(candidates.shape[0], dtype=jnp.int32)[None, :] == targets[:, None]).astype(jnp.float32)
        losses = log_total[:, 0] - lax.optimization_barrier(jnp.sum(scores * onehot, axis=1))
        score_grad = (sharpness * (jnp.exp(scores - log_total) - onehot) / QUERIES).astype(jnp.bfloat16)
        query_grad = jnp.dot(score_grad, candidates, preferred_element_type=jnp.float32)
        cand_grad = jnp.dot(score_grad.T, queries, preferred_element_type=jnp.float32)
        return (losses, query_grad, cand_grad[:pass_rows], cand_grad[pass_rows:].astype(jnp.bfloat16), starts)
    losses, query_grad, near_grad, far_grad, starts = lax.map(one_device, jnp.arange(devices, dtype=jnp.int32))
    offsets = (starts[:, :, None] + jnp.arange(BLOCK, dtype=jnp.int32)[None, None, :]).reshape(-1)
    passage_grad = near_grad.reshape(PASSAGES, D).at[offsets].add(far_grad.reshape(-1, D).astype(jnp.float32))
    query_delta = unembed(query_grad.reshape(QUERIES, D), query_unit, query_factor)
    passage_delta = unembed(passage_grad, passage_unit, passage_factor)
    contract = (((1,), (1,)), ((), ()))
    query_back = lax.dot_general(query_delta, out_weight, contract, preferred_element_type=jnp.float32).astype(jnp.bfloat16)
    passage_back = lax.dot_general(passage_delta, out_weight, contract, preferred_element_type=jnp.float32).astype(jnp.bfloat16)

    def accumulate(running, device):
        attend = jnp.concatenate([lax.dynamic_slice_in_dim(query_attn, device * BLOCK, BLOCK, 0), lax.dynamic_slice_in_dim(passage_attn, device * pass_rows, pass_rows, 0)], axis=0)
        deltas = jnp.concatenate([lax.dynamic_slice_in_dim(query_delta, device * BLOCK, BLOCK, 0), lax.dynamic_slice_in_dim(passage_delta, device * pass_rows, pass_rows, 0)], axis=0)
        partial_value = lax.dot_general(attend, deltas, (((0,), (0,)), ((), ())), preferred_element_type=jnp.float32)
        partial_value = lax.optimization_barrier(partial_value.astype(jnp.bfloat16)).astype(jnp.float32)
        return (running + partial_value, None)
    weight_grad, unused = lax.scan(accumulate, jnp.zeros((HD, D), jnp.float32), jnp.arange(devices, dtype=jnp.int32))
    return (losses.reshape(QUERIES), query_back, query_delta, passage_back, passage_delta, weight_grad)
```

```python
import jax
import jax.numpy as jnp
from jax import lax
from jax.experimental import pallas as pl
from jax.experimental.pallas import tpu as pltpu
from jax.sharding import PartitionSpec as P

BLOCK = 128
SIDE = 4
CORES = 2
FSDP = SIDE * SIDE * CORES
DEVICES = SIDE * FSDP

sharpness = 250.0
epsilon = 1e-06
BF = jnp.bfloat16
F32 = jnp.float32


def route(target):
    pairs = []
    for source in range(DEVICES):
        z, rest = divmod(source, FSDP)
        y, rest = divmod(rest, SIDE * CORES)
        x, c = divmod(rest, CORES)
        z, y, x, c = target(z, y, x, c)
        pairs.append((source, (((z % SIDE) * SIDE + y % SIDE) * SIDE + x % SIDE) * CORES + c))
    return lambda value: lax.ppermute(value, ("dp", "fsdp"), pairs)


def way(c):
    return 1 - 2 * c


swap = route(lambda z, y, x, c: (z, y, x, 1 - c))
x_ring = route(lambda z, y, x, c: (z, y, x + way(c), c))
y_ring = route(lambda z, y, x, c: (z, y + way(c), x, c))
z_ring = route(lambda z, y, x, c: (z + way(c), y, x, c))
x_back = [route(lambda z, y, x, c, k=k: (z, y, x - k, c)) for k in range(SIDE)]
y_back = [route(lambda z, y, x, c, k=k: (z, y - k, x, c)) for k in range(SIDE)]
x_on = [route(lambda z, y, x, c, k=k: (z, y, x + k, c)) for k in range(SIDE)]
y_on = [route(lambda z, y, x, c, k=k: (z, y + k, x, c)) for k in range(SIDE)]
z_on = [route(lambda z, y, x, c, k=k: (z + way(c) * k, y, x, c)) for k in range(SIDE)]


def dot(a, b, dims, batch=((), ())):
    return lax.dot_general(a, b, (dims, batch), preferred_element_type=F32)


ROW_TILE = 224
MIB = 1024 * 1024
ANYWHERE = pl.BlockSpec(memory_space=pl.ANY)
SCALARS = pl.BlockSpec(memory_space=pltpu.SMEM)
NT = ((1,), (1,))
NN = ((1,), (0,))
TN = ((0,), (0,))


def cost(flops, traffic):
    return pl.CostEstimate(flops=int(flops), bytes_accessed=int(traffic), transcendentals=0)


def whole(shape):
    return pl.BlockSpec(shape, lambda *_: (0,) * len(shape))


def copy_kernel(core_ref, in_ref, out_ref):
    out_ref[...] = in_ref[...]


def other_half(core, rows):
    height, half = rows.shape[0], rows.shape[1] // 2
    return pl.pallas_call(
        copy_kernel,
        out_shape=jax.ShapeDtypeStruct((height, half), rows.dtype),
        grid_spec=pltpu.PrefetchScalarGridSpec(
            num_scalar_prefetch=1,
            grid=(1,),
            in_specs=[pl.BlockSpec((height, half), lambda i, core: (0, 1 - core[0]))],
            out_specs=pl.BlockSpec((height, half), lambda i, core: (0, 0)),
        ),
        compiler_params=pltpu.CompilerParams(vmem_limit_bytes=8 * MIB),
        cost_estimate=cost(0, 4 * height * half),
        name="other_half",
    )(core, rows)


def shard_kernel(core_ref, own_ref, got_ref, a_ref, b_ref):
    core = core_ref[0]
    height, half = own_ref.shape
    quarter = half // 2
    for rows, at in ((own_ref, core), (got_ref, 1 - core)):
        place = pl.ds(pl.multiple_of(at * height, height), height)
        a_ref[place, :] = rows[:, :quarter]
        b_ref[place, :] = rows[:, quarter:]


def chip_shard(core, weight, got):
    height, half = got.shape
    part = jax.ShapeDtypeStruct((CORES * height, half // 2), weight.dtype)
    return pl.pallas_call(
        shard_kernel,
        out_shape=(part, part),
        grid_spec=pltpu.PrefetchScalarGridSpec(
            num_scalar_prefetch=1,
            grid=(1,),
            in_specs=[pl.BlockSpec((height, half), lambda i, core: (0, core[0])), whole(got.shape)],
            out_specs=(whole(part.shape), whole(part.shape)),
        ),
        compiler_params=pltpu.CompilerParams(vmem_limit_bytes=8 * MIB),
        cost_estimate=cost(0, 8 * height * half),
        name="chip_shard",
    )(core, weight, got)


def pair_rows_kernel(core_ref, own_ref, got_ref, out_ref):
    height = own_ref.shape[0]
    out_ref[:height] = own_ref[...]
    out_ref[height:] = got_ref[...]


def pair_rows(core, rows, got):
    height, half = got.shape
    return pl.pallas_call(
        pair_rows_kernel,
        out_shape=jax.ShapeDtypeStruct((CORES * height, half), rows.dtype),
        grid_spec=pltpu.PrefetchScalarGridSpec(
            num_scalar_prefetch=1,
            grid=(1,),
            in_specs=[pl.BlockSpec((height, half), lambda i, core: (0, core[0])), whole(got.shape)],
            out_specs=whole((CORES * height, half)),
        ),
        compiler_params=pltpu.CompilerParams(vmem_limit_bytes=8 * MIB),
        cost_estimate=cost(0, 8 * height * half),
        name="pair_rows",
    )(core, rows, got)


def columns(order_ref, which, i):
    return pl.ds(pl.multiple_of(order_ref[which, i] * BLOCK, BLOCK), BLOCK)


def contract_kernel(steps, places, order_ref, *refs):
    count = len(places)
    pieces, weights = refs[:count], refs[count : count + 2 * steps]
    total_ref, rows_ref, held, sems = refs[count + 2 * steps :]
    i = pl.program_id(0)
    copies = [
        pltpu.make_async_copy(piece, held.at[pl.ds(at, piece.shape[0]), :], sems.at[n])
        for n, (piece, at) in enumerate(zip(pieces, places))
    ]
    early = [n for n, at in enumerate(places) if at < held.shape[0] // CORES]

    @pl.when(i == 0)
    def _():
        for copy in copies:
            copy.start()
        for n in early:
            copies[n].wait()

    @pl.when(i == pl.num_programs(0) // CORES)
    def _():
        for n in range(count):
            if n not in early:
                copies[n].wait()

    rows = pl.ds(pl.multiple_of(i * ROW_TILE, ROW_TILE), ROW_TILE)
    rows_ref[...] = held[rows, :]
    quarter = total_ref.shape[1] // 2
    for which in range(2):
        total = None
        for j in range(steps):
            left = jnp.concatenate(
                [held[rows, columns(order_ref, which, j * SIDE + k)] for k in range(SIDE)], axis=1
            )
            part = dot(left, weights[which * steps + j][...], NN)
            total = part if total is None else total + part
        total_ref[:, which * quarter : (which + 1) * quarter] = total


def contract(order, pieces, places, a_parts, b_parts):
    height = places[-1] + pieces[-1].shape[0]
    depth = pieces[0].shape[1]
    block, quarter = a_parts[0].shape
    steps = len(a_parts)
    return pl.pallas_call(
        lambda *refs: contract_kernel(steps, places, *refs),
        out_shape=(
            jax.ShapeDtypeStruct((height, 2 * quarter), F32),
            jax.ShapeDtypeStruct((height, depth), BF),
        ),
        grid=(height // ROW_TILE,),
        in_specs=[SCALARS]
        + [ANYWHERE] * len(pieces)
        + [whole((block, quarter))] * (2 * steps),
        out_specs=(
            pl.BlockSpec((ROW_TILE, 2 * quarter), lambda i: (i, 0)),
            pl.BlockSpec((ROW_TILE, depth), lambda i: (i, 0)),
        ),
        scratch_shapes=[
            pltpu.VMEM((height, depth), BF),
            pltpu.SemaphoreType.DMA((len(pieces),)),
        ],
        compiler_params=pltpu.CompilerParams(vmem_limit_bytes=40 * MIB),
        cost_estimate=cost(
            2 * height * steps * block * 2 * quarter, height * (depth * 4 + quarter * 8)
        ),
        name="contract",
    )(order, *pieces, *a_parts, *b_parts)


def mix_kernel(places, order_ref, core_ref, total_ref, *refs):
    lefts, refs = refs[: 2 * SIDE], refs[2 * SIDE :]
    weights, refs = refs[:2], refs[2:]
    count = len(places)
    pieces, refs = refs[:count], refs[count:]
    low_ref, raw_ref, square_ref, held, lows, sems = refs
    i = pl.program_id(0)
    half = held.shape[1]
    per_core = lows.shape[0]
    tiles = per_core // ROW_TILE
    copies = []
    for n, (source, take, at, high) in enumerate(places):
        piece = pieces[n]
        if source:
            piece = piece.at[:, pl.ds(pl.multiple_of(core_ref[0] * half, half), half)]
        else:
            piece = piece.at[pl.ds(take, high), :]
        copies.append(
            pltpu.make_async_copy(piece, held.at[pl.ds(at, high), :], sems.at[n])
        )
    early = [n for n, place in enumerate(places) if place[2] < per_core]

    @pl.when(i == 0)
    def _():
        for copy in copies:
            copy.start()
        for n in early:
            copies[n].wait()

    @pl.when(i == tiles)
    def _():
        for n in range(count):
            if n not in early:
                copies[n].wait()

    rows = pl.ds(pl.multiple_of(i * ROW_TILE, ROW_TILE), ROW_TILE)
    inside = pl.ds(pl.multiple_of((i % tiles) * ROW_TILE, ROW_TILE), ROW_TILE)
    quarter = half // 2
    squares = None
    for which in range(2):
        cols = slice(which * quarter, (which + 1) * quarter)
        left = jnp.concatenate(
            [lefts[which * SIDE + k][...] for k in range(SIDE)], axis=1
        )
        mixed = total_ref[:, cols] + held[rows, cols].astype(F32)
        mixed = mixed + dot(left, weights[which][...], NN)
        low = mixed.astype(BF)
        low_ref[:, cols] = low
        lows[inside, cols] = low
        part = jnp.sum(mixed * mixed, axis=1, keepdims=True)
        squares = part if squares is None else squares + part
    square_ref[...] = jnp.broadcast_to(squares, square_ref.shape)

    @pl.when(i % tiles == tiles - 1)
    def _():
        own = raw_ref.shape[2]
        raw_ref[0] = dot(lows[own:, :], lows[:own, :], NT)


def mix(order, core, total, rows, a_part, b_part, pieces, places, own_rows):
    height, half = total.shape
    per_core = height // CORES
    tiles = per_core // ROW_TILE
    last = (SIDE - 1) * SIDE
    tile = lambda width: pl.BlockSpec((ROW_TILE, width), lambda i, *_: (i, 0))
    lefts = [
        pl.BlockSpec((ROW_TILE, BLOCK), lambda i, o, core, w=w, k=k: (i, o[w, last + k]))
        for w in range(2)
        for k in range(SIDE)
    ]
    queries = per_core - own_rows
    return pl.pallas_call(
        lambda *refs: mix_kernel(places, *refs),
        out_shape=(
            jax.ShapeDtypeStruct((height, half), BF),
            jax.ShapeDtypeStruct((CORES, queries, own_rows), F32),
            jax.ShapeDtypeStruct((height, BLOCK), F32),
        ),
        grid_spec=pltpu.PrefetchScalarGridSpec(
            num_scalar_prefetch=2,
            grid=(height // ROW_TILE,),
            in_specs=[tile(half)]
            + lefts
            + [whole(a_part.shape)] * 2
            + [ANYWHERE] * len(pieces),
            out_specs=(
                tile(half),
                pl.BlockSpec((1, queries, own_rows), lambda i, *_: (i // tiles, 0, 0)),
                tile(BLOCK),
            ),
            scratch_shapes=[
                pltpu.VMEM((height, half), BF),
                pltpu.VMEM((per_core, half), BF),
                pltpu.SemaphoreType.DMA((len(pieces),)),
            ],
        ),
        compiler_params=pltpu.CompilerParams(vmem_limit_bytes=40 * MIB),
        cost_estimate=cost(2 * height * 1024 * half, height * half * 10),
        name="mix",
    )(order, core, total, *([rows] * (2 * SIDE)), a_part, b_part, *pieces)


def project_kernel(low_ref, grad_q_ref, grad_p_ref, coef_ref, delta_ref):
    own = grad_q_ref.shape[2]
    low_p, low_q = low_ref[0, :own], low_ref[0, own:]
    up_p = dot(grad_p_ref[0], low_q, TN)
    delta_ref[0, 0, :own] = (
        up_p * coef_ref[0, :own, 0:1] - low_p.astype(F32) * coef_ref[0, :own, 1:2]
    ).astype(BF)
    up_q = dot(grad_q_ref[0], low_p, NN)
    delta_ref[0, 0, own:] = (
        up_q * coef_ref[0, own:, 0:1] - low_q.astype(F32) * coef_ref[0, own:, 1:2]
    ).astype(BF)


def project(low, grad_q, grad_p, coef):
    cores, per_core, half = low.shape
    quarter = half // 2
    scores = pl.BlockSpec((1,) + grad_q.shape[1:], lambda h, e: (e, 0, 0))
    return pl.pallas_call(
        project_kernel,
        out_shape=jax.ShapeDtypeStruct((2, cores, per_core, quarter), BF),
        grid=(2, cores),
        in_specs=[
            pl.BlockSpec((1, per_core, quarter), lambda h, e: (e, 0, h)),
            scores,
            scores,
            pl.BlockSpec((1, per_core, 2), lambda h, e: (e, 0, 0)),
        ],
        out_specs=pl.BlockSpec((1, 1, per_core, quarter), lambda h, e: (h, e, 0, 0)),
        compiler_params=pltpu.CompilerParams(vmem_limit_bytes=32 * MIB),
        cost_estimate=cost(4 * grad_q.size * half, low.size * 4),
        name="project",
    )(low, grad_q, grad_p, coef)


def term_kernel(order_ref, *refs):
    lefts, refs = refs[:SIDE], refs[SIDE:]
    delta_ref, refs = refs[0], refs[1:]
    out_ref, turned = refs[-2:]

    @pl.when(pl.program_id(0) == 0)
    def _():
        for k in range(SIDE):
            turned[k * BLOCK : (k + 1) * BLOCK, :] = lefts[k][...].T

    value = dot(turned[...], delta_ref[0], NN)
    if len(refs) == 3:
        value = value + refs[0][...].astype(F32)
    out_ref[...] = value.astype(BF)


def term(order, rows, delta, which, j, moving=None):
    height, quarter = delta.shape[1:]
    slab = quarter // 4
    out = pl.BlockSpec((SIDE * BLOCK, slab), lambda i, o: (0, i))
    lefts = [
        pl.BlockSpec((height, BLOCK), lambda i, o, k=k: (0, o[which, j * SIDE + k]))
        for k in range(SIDE)
    ]
    return pl.pallas_call(
        term_kernel,
        out_shape=jax.ShapeDtypeStruct((SIDE * BLOCK, quarter), BF),
        grid_spec=pltpu.PrefetchScalarGridSpec(
            num_scalar_prefetch=1,
            grid=(4,),
            in_specs=lefts
            + [pl.BlockSpec((1, height, slab), lambda i, o: (which, 0, i))]
            + ([] if moving is None else [out]),
            out_specs=out,
            scratch_shapes=[pltpu.VMEM((SIDE * BLOCK, height), BF)],
        ),
        compiler_params=pltpu.CompilerParams(vmem_limit_bytes=24 * MIB),
        cost_estimate=cost(2 * height * SIDE * BLOCK * quarter, height * (quarter + 512) * 2),
        name="term",
    )(order, *([rows] * SIDE), delta, *(() if moving is None else (moving,)))


def back_kernel(order_ref, a_ref, b_ref, *refs):
    weights, (own_ref, other_ref, held) = refs[: 2 * SIDE], refs[2 * SIDE :]
    for which, rows in enumerate((a_ref, b_ref)):
        left = rows[...].reshape(held.shape[0], rows.shape[-1])
        for j in range(SIDE):
            value = dot(left, weights[which * SIDE + j][...], NT)
            for k in range(SIDE):
                place = columns(order_ref, which, j * SIDE + k)
                piece = value[:, k * BLOCK : (k + 1) * BLOCK]
                held[:, place] = piece if which == 0 else held[:, place] + piece

    @pl.when(pl.program_id(0) == 0)
    def _():
        own_ref[...] = held[...]

    @pl.when(pl.program_id(0) == 1)
    def _():
        other_ref[...] = held[...].astype(BF)


def back(order, delta, height, a_parts, b_parts):
    block, quarter = a_parts[0].shape
    depth = SIDE * block
    lefts = [
        pl.BlockSpec((1, 1, height, quarter), lambda e, h=h: (h, e, 0, 0)) for h in range(2)
    ]
    return pl.pallas_call(
        back_kernel,
        out_shape=(
            jax.ShapeDtypeStruct((height, depth), F32),
            jax.ShapeDtypeStruct((height, depth), BF),
        ),
        grid=(CORES,),
        in_specs=[SCALARS] + lefts + [whole((block, quarter))] * (2 * SIDE),
        out_specs=(whole((height, depth)), whole((height, depth))),
        scratch_shapes=[pltpu.VMEM((height, depth), F32)],
        compiler_params=pltpu.CompilerParams(vmem_limit_bytes=40 * MIB),
        cost_estimate=cost(8 * CORES * height * depth * quarter, 16 * MIB),
        name="back",
    )(order, delta, delta, *a_parts, *b_parts)


def lay_kernel(core_ref, own_ref, got_ref, out_ref):
    i = pl.program_id(0)

    @pl.when(i < 2)
    def _():
        out_ref[...] = own_ref[0, 0]

    @pl.when(i >= 2)
    def _():
        out_ref[...] = got_ref[0]


def lay(core, delta, got):
    _, height, quarter = got.shape
    return pl.pallas_call(
        lay_kernel,
        out_shape=jax.ShapeDtypeStruct((height, 4 * quarter), BF),
        grid_spec=pltpu.PrefetchScalarGridSpec(
            num_scalar_prefetch=1,
            grid=(4,),
            in_specs=[
                pl.BlockSpec(
                    (1, 1, height, quarter), lambda i, core: (jnp.minimum(i, 1), 0, 0, 0)
                ),
                pl.BlockSpec((1, height, quarter), lambda i, core: (jnp.maximum(i - 2, 0), 0, 0)),
            ],
            out_specs=pl.BlockSpec(
                (height, quarter),
                lambda i, core: (0, jnp.where(i < 2, 2 * core[0], 2 * (1 - core[0]) - 2) + i),
            ),
        ),
        compiler_params=pltpu.CompilerParams(vmem_limit_bytes=16 * MIB),
        cost_estimate=cost(0, 16 * height * quarter),
        name="lay",
    )(core, delta, got)


def flipped(value):
    order = [value[:, (SIDE - j) % SIDE] for j in range(SIDE)]
    return jnp.stack(order, axis=1)[::-1]


def body(query_attn, query_resid, passage_attn, passage_resid, out_weight, hard_lists, positive):
    z = lax.axis_index("dp")
    f = lax.axis_index("fsdp")
    c, x, y = f % CORES, (f // CORES) % SIDE, f // (SIDE * CORES)
    step = 1 - 2 * c
    first = c == 0
    width = query_resid.shape[1]
    half = width // 2
    quarter = half // 2
    own_rows = passage_attn.shape[0]
    blocks = own_rows // BLOCK

    core = c.astype(jnp.int32).reshape(1)
    per_core = own_rows + SIDE * BLOCK

    shard_a, shard_b = chip_shard(core, out_weight, swap(other_half(core, out_weight)))
    near_a = {k: x_back[k](shard_a) for k in (1, 3, 2)}
    near_b = {k: y_back[k](shard_b) for k in (1, 3, 2)}
    a_parts = [jnp.concatenate([shard_a] + [near_a[k] for k in (1, 2, 3)], axis=0)]
    b_parts = [jnp.concatenate([shard_b] + [near_b[k] for k in (1, 2, 3)], axis=0)]
    for j in range(1, SIDE):
        a_parts.append(y_ring(a_parts[-1]))
        b_parts.append(x_ring(b_parts[-1]))
    ks = jnp.arange(SIDE, dtype=jnp.int32)
    a_order = (((y - step * ks) % SIDE)[:, None] * SIDE + ((x + ks) % SIDE)[None, :]).reshape(-1)
    b_order = (((y + ks) % SIDE)[None, :] * SIDE + ((x - step * ks) % SIDE)[:, None]).reshape(-1)
    order = jnp.stack([a_order, b_order]).astype(jnp.int32)

    attn_z = [query_attn]
    for j in range(1, SIDE):
        attn_z.append(z_ring(attn_z[-1]))
    attn_p = [swap(v) for v in attn_z]
    attn_p = [attn_p[(SIDE - j) % SIDE] for j in range(SIDE)]
    resid_z = [pair_rows(core, query_resid, swap(other_half(core, query_resid)))]
    for j in range(1, SIDE):
        resid_z.append(z_ring(resid_z[-1]))

    pieces = [passage_attn] + attn_z + [swap(passage_attn)] + attn_p
    places, at = [], 0
    for v in pieces:
        places.append(at)
        at += v.shape[0]
    total, rows = contract(order, pieces, places, a_parts[:-1], b_parts[:-1])

    pieces = [passage_resid] + resid_z + [swap(other_half(core, passage_resid))] + resid_z
    places = [(True, 0, 0, own_rows)]
    places += [(False, 0, own_rows + j * BLOCK, BLOCK) for j in range(SIDE)]
    places += [(False, 0, per_core, own_rows)]
    places += [(False, BLOCK, per_core + own_rows + j * BLOCK, BLOCK) for j in range(SIDE)]
    low, raw, squares = mix(
        order, core, total, rows, a_parts[-1], b_parts[-1], pieces, places, own_rows
    )
    squares = squares[:, 0]
    low = low.reshape(CORES, per_core, half)
    raw = raw.reshape(CORES, SIDE, BLOCK, own_rows)

    squares = squares.reshape(CORES, per_core)
    squares_p = squares[:, :own_rows]
    squares_q = squares[:, own_rows:].reshape(CORES, SIDE, BLOCK)
    packed = jnp.concatenate([squares_p.reshape(-1), squares_q.reshape(-1)])
    other = swap(packed)
    split = CORES * own_rows
    squares_p = squares_p + other[:split].reshape(CORES, own_rows)[::-1]
    squares_q = squares_q + flipped(other[split:].reshape(CORES, SIDE, BLOCK))
    raw = raw + flipped(swap(raw))
    factor_p = lax.rsqrt(squares_p + epsilon)
    factor_q = lax.rsqrt(squares_q + epsilon)

    lists = jnp.stack([hard_lists[0], swap(hard_lists[0])])
    source = (z - step * ks) % SIDE
    asked = jnp.take(lists, source, axis=1)
    ids = z * blocks + jnp.arange(blocks, dtype=jnp.int32)
    wanted = jnp.any(asked[:, :, :, None] == ids, axis=2)
    wanted = wanted | (ks == 0)[None, :, None]
    wanted = jnp.repeat(wanted, BLOCK, axis=2)[:, :, None, :]
    hits = jnp.stack([positive, swap(positive)])
    target = (jnp.arange(own_rows, dtype=jnp.int32) == hits[:, :, None])[:, None]
    target = (target & (ks == 0)[None, :, None, None]).astype(F32)

    scores = sharpness * raw * factor_q[..., None] * factor_p[:, None, None, :]
    scores = jnp.where(wanted, scores, -1e30)
    highest = jnp.max(scores, axis=3)
    totals = jnp.sum(jnp.exp(scores - highest[..., None]), axis=3)
    stats = jnp.stack([highest, totals])
    all_stats = [stats]
    for k in range(1, SIDE):
        got = z_on[k](stats)
        all_stats.append(jnp.concatenate([got[:, :, SIDE - k :], got[:, :, : SIDE - k]], axis=2))
    top = all_stats[0][0]
    for v in all_stats[1:]:
        top = jnp.maximum(top, v[0])
    log_total = top + jnp.log(sum(v[1] * jnp.exp(v[0] - top) for v in all_stats))
    query_loss = log_total[0, 0] - jnp.sum(scores[0, 0] * target[0, 0], axis=1)

    scale = sharpness / (BLOCK * DEVICES)
    grad = scale * (jnp.exp(scores - log_total[..., None]) - target)
    weighted = grad * scores * (1.0 / sharpness)
    inner_q = jnp.sum(weighted, axis=3)
    inner_p = jnp.sum(weighted, axis=(1, 2))
    grad_q = (grad * factor_p[:, None, None, :]).astype(BF).reshape(CORES, -1, own_rows)
    grad_p = (grad * factor_q[..., None]).astype(BF).reshape(CORES, -1, own_rows)
    factors = jnp.concatenate([factor_p, factor_q.reshape(CORES, -1)], axis=1)
    inners = jnp.concatenate([inner_p, inner_q.reshape(CORES, -1)], axis=1)
    coef = jnp.stack([factors, factors * factors * inners], axis=2)
    delta = project(low, grad_q, grad_p, coef)
    flat = delta.reshape(2, CORES * per_core, quarter)

    moving = [term(order, rows, flat, i, 1) for i in range(2)]
    for j in (2, 3, 0):
        moving = [y_ring(moving[0]), x_ring(moving[1])]
        moving = [term(order, rows, flat, i, j, moving[i]) for i in range(2)]
    sums = []
    for i, send in enumerate((x_on, y_on)):
        parts = [moving[i][k * BLOCK : (k + 1) * BLOCK] for k in range(SIDE)]
        got = [parts[0]] + [send[k](parts[k]) for k in (1, 3, 2)]
        sums.append(sum(v.astype(F32) for v in got).astype(BF))
    part = jnp.concatenate(sums, axis=1).reshape(CORES, SIDE, BLOCK // 8, half)

    def pick(v, index, axis):
        return lax.dynamic_index_in_dim(v, index, axis, keepdims=False)

    total = pick(part, z, 1).astype(F32)
    for k in (1, 3, 2):
        total = total + z_on[k](pick(part, (z + step * k) % SIDE, 1)).astype(F32)
    total = total.astype(BF)
    own, other = pick(total, c, 0), swap(pick(total, 1 - c, 0))
    total = jnp.where(
        first, jnp.concatenate([own, other], axis=1), jnp.concatenate([other, own], axis=1)
    )
    weight_grad = jnp.zeros((SIDE,) + total.shape, F32)
    for k in (0, 1, 3, 2):
        got = total if k == 0 else z_on[k](total)
        weight_grad = lax.dynamic_update_index_in_dim(
            weight_grad, got.astype(F32), (z - step * k) % SIDE, 0
        )
    weight_grad = weight_grad.reshape(out_weight.shape)

    def part_of(j):
        return delta[:, :, own_rows + j * BLOCK : own_rows + (j + 1) * BLOCK]

    travelling = part_of(1)
    for j in (2, 3, 0):
        travelling = (z_ring(travelling).astype(F32) + part_of(j).astype(F32)).astype(BF)

    def finish(rows, height):
        own, other = back(order, rows, height, a_parts, b_parts)
        value = (own + swap(other).astype(F32)).astype(BF)
        return value, lay(core, rows, swap(rows[:, 1, :height]))

    passage_back, passage_delta = finish(delta, own_rows)
    query_back, query_delta = finish(travelling, BLOCK)
    return (query_loss, query_back, query_delta, passage_back, passage_delta, weight_grad)


def solution(mesh):
    rows = P(("dp", "fsdp"), None)
    return jax.shard_map(
        body,
        mesh=mesh,
        in_specs=(
            rows,
            rows,
            rows,
            rows,
            P("fsdp", None),
            P("fsdp", None, None),
            P(("dp", "fsdp")),
        ),
        out_specs=(P(("dp", "fsdp")), rows, rows, rows, rows, P("fsdp", None)),
        check_vma=False,
    )
```

```python
import jax
import jax.numpy as jnp
from jax import lax
from jax.experimental import pallas as pl
from jax.experimental.pallas import tpu as pltpu
from jax.sharding import PartitionSpec as P

BLOCK = 128
SIDE = 4
CORES = 2
FSDP = SIDE * SIDE * CORES
DEVICES = SIDE * FSDP

sharpness = 250.0
epsilon = 1e-06
BF = jnp.bfloat16
F32 = jnp.float32


def route(target):
    pairs = []
    for source in range(DEVICES):
        z, rest = divmod(source, FSDP)
        y, rest = divmod(rest, SIDE * CORES)
        x, c = divmod(rest, CORES)
        z, y, x, c = target(z, y, x, c)
        pairs.append((source, (((z % SIDE) * SIDE + y % SIDE) * SIDE + x % SIDE) * CORES + c))
    return lambda value: lax.ppermute(value, ("dp", "fsdp"), pairs)


def way(c):
    return 1 - 2 * c


def along_first(shift):
    return route(
        lambda z, y, x, c: (z, y, x + shift, c) if c == 0 else (z, y + shift, x, c)
    )


def along_second(shift):
    return route(
        lambda z, y, x, c: (z, y + shift, x, c) if c == 0 else (z, y, x + shift, c)
    )


swap = route(lambda z, y, x, c: (z, y, x, 1 - c))
z_to = [route(lambda z, y, x, c, k=k: (z + k, y, x, c)) for k in range(SIDE)]
z_up, z_across, z_down = z_to[1:]
z_with = route(lambda z, y, x, c: (z + way(c), y, x, c))
z_against = route(lambda z, y, x, c: (z - way(c), y, x, c))
first_up, first_down, first_across = (along_first(shift) for shift in (1, -1, 2))
second_up, second_down = (along_second(shift) for shift in (1, -1))


def dot(a, b, dims, batch=((), ())):
    return lax.dot_general(a, b, (dims, batch), preferred_element_type=F32)


TALL_TILE = 256
MIB = 1024 * 1024
HOPS = (0, -1, 1, 2)
ANYWHERE = pl.BlockSpec(memory_space=pl.ANY)
SCALARS = pl.BlockSpec(memory_space=pltpu.SMEM)
NT = ((1,), (1,))
NN = ((1,), (0,))
TN = ((0,), (0,))


def cost(flops, traffic):
    return pl.CostEstimate(
        flops=int(flops) // 4, bytes_accessed=int(traffic) // 4, transcendentals=0
    )


def room(mib):
    return pltpu.CompilerParams(vmem_limit_bytes=mib * MIB)


def whole(shape):
    return pl.BlockSpec(shape, lambda *_: (0,) * len(shape), pipeline_mode=pl.Buffered(1))


MARK = (8, BLOCK)
MARKED = jax.ShapeDtypeStruct(MARK, F32)


def copy_kernel(core_ref, in_ref, *refs):
    refs[-1][...] = in_ref[...]


def other_half(core, rows, after=()):
    height, half = rows.shape[0], rows.shape[1] // 2
    return pl.pallas_call(
        copy_kernel,
        out_shape=jax.ShapeDtypeStruct((height, half), rows.dtype),
        grid_spec=pltpu.PrefetchScalarGridSpec(
            num_scalar_prefetch=1,
            grid=(1,),
            in_specs=[pl.BlockSpec((height, half), lambda i, core: (0, 1 - core[0]))]
            + [ANYWHERE] * len(after),
            out_specs=pl.BlockSpec((height, half), lambda i, core: (0, 0)),
        ),
        compiler_params=room(12),
        cost_estimate=cost(0, 4 * height * half),
        name="other_half",
    )(core, rows, *after)


def halves_of_kernel(core_ref, *refs):
    at = 0
    for ref in refs[:-1]:
        refs[-1][at : at + ref.shape[0]] = ref[...]
        at += ref.shape[0]


def other_halves(core, arrays):
    half = arrays[0].shape[1] // 2
    shape = (sum(v.shape[0] for v in arrays), half)
    return pl.pallas_call(
        halves_of_kernel,
        out_shape=jax.ShapeDtypeStruct(shape, BF),
        grid_spec=pltpu.PrefetchScalarGridSpec(
            num_scalar_prefetch=1,
            grid=(1,),
            in_specs=[
                pl.BlockSpec((v.shape[0], half), lambda i, core: (0, 1 - core[0])) for v in arrays
            ],
            out_specs=whole(shape),
        ),
        compiler_params=room(8),
        cost_estimate=cost(0, 4 * shape[0] * half),
        name="other_halves",
    )(core, *arrays)


def shard_kernel(core_ref, own_ref, got_ref, out_ref):
    core = core_ref[0]
    height = own_ref.shape[0]
    for rows, at in ((own_ref, core), (got_ref, 1 - core)):
        out_ref[pl.ds(pl.multiple_of(at * height, height), height), :] = rows[:height]


def chip_shard(core, weight, got):
    height, half = weight.shape[0], got.shape[1]
    return pl.pallas_call(
        shard_kernel,
        out_shape=jax.ShapeDtypeStruct((CORES * height, half), weight.dtype),
        grid_spec=pltpu.PrefetchScalarGridSpec(
            num_scalar_prefetch=1,
            grid=(1,),
            in_specs=[
                pl.BlockSpec((height, half), lambda i, core: (0, core[0])),
                whole(got.shape),
            ],
            out_specs=whole((CORES * height, half)),
        ),
        compiler_params=room(12),
        cost_estimate=cost(0, 8 * height * half),
        name="chip_shard",
    )(core, weight, got)


def pair_rows_kernel(core_ref, own_ref, got_ref, out_ref):
    height = own_ref.shape[0]
    out_ref[:height] = own_ref[...]
    out_ref[height:] = got_ref[got_ref.shape[0] - height :]


def pair_rows(core, rows, got):
    height, half = rows.shape[0], got.shape[1]
    return pl.pallas_call(
        pair_rows_kernel,
        out_shape=jax.ShapeDtypeStruct((CORES * height, half), rows.dtype),
        grid_spec=pltpu.PrefetchScalarGridSpec(
            num_scalar_prefetch=1,
            grid=(1,),
            in_specs=[pl.BlockSpec((height, half), lambda i, core: (0, core[0])), whole(got.shape)],
            out_specs=whole((CORES * height, half)),
        ),
        compiler_params=room(12),
        cost_estimate=cost(0, 8 * height * half),
        name="pair_rows",
    )(core, rows, got)


def columns(order_ref, i):
    return pl.ds(pl.multiple_of(order_ref[i] * BLOCK, BLOCK), BLOCK)


def pack_kernel(near, *refs):
    count = len(near)
    rows, (attn_ref, up_ref, down_ref, resid_ref) = refs[:count], refs[count : count + 4]
    weight_ref, to_up, to_down, three_ref = refs[-4:]
    for n, row in enumerate(rows):
        weight_ref[n * BLOCK : (n + 1) * BLOCK] = row[...]
    part = BLOCK // 2
    to_up[:part] = up_ref[:part]
    to_up[part:] = resid_ref[...]
    to_down[:part] = down_ref[part:]
    to_down[part:] = resid_ref[...]
    for n, row in enumerate((attn_ref, up_ref, down_ref)):
        three_ref[n * BLOCK : (n + 1) * BLOCK] = row[...]


def pack(near, attn, up, down, resid):
    half = near[0].shape[1]
    height = BLOCK // 2 + resid.shape[0]
    shapes = [(SIDE * BLOCK, half), (height, half), (height, half), (3 * BLOCK, half)]
    operands = [*near, attn, up, down, resid]
    return pl.pallas_call(
        lambda *refs: pack_kernel(near, *refs),
        out_shape=[jax.ShapeDtypeStruct(s, BF) for s in shapes],
        grid=(1,),
        in_specs=[whole(v.shape) for v in operands],
        out_specs=[whole(s) for s in shapes],
        compiler_params=room(16),
        cost_estimate=cost(0, 12 * MIB),
        name="pack",
    )(*operands)


def halves_kernel(one_ref, two_ref, *refs):
    refs[-2][...] = one_ref[...]
    refs[-1][...] = two_ref[...]


def halves(one, two, after):
    height, half = one.shape
    shape = (height // 2, half)
    return pl.pallas_call(
        halves_kernel,
        out_shape=[jax.ShapeDtypeStruct(shape, BF)] * 2,
        grid=(1,),
        in_specs=[
            pl.BlockSpec(shape, lambda i: (0, 0)),
            pl.BlockSpec(shape, lambda i: (1, 0)),
        ]
        + [whole(MARK)] * len(after),
        out_specs=[whole(shape)] * 2,
        compiler_params=room(16),
        cost_estimate=cost(0, 8 * MIB),
        name="halves",
    )(one, two, *after)


def repack_kernel(up_ref, down_ref, *refs):
    outs = refs[-3:]
    part = BLOCK // 2
    outs[0][...] = up_ref[part : part + BLOCK]
    outs[1][...] = down_ref[part + BLOCK :]
    outs[2][:part] = up_ref[:part]
    outs[2][part:] = down_ref[:part]


def repack(up, down, after):
    shape = (BLOCK, up.shape[1])
    return pl.pallas_call(
        repack_kernel,
        out_shape=[jax.ShapeDtypeStruct(shape, BF)] * 3,
        grid=(1,),
        in_specs=[whole(up.shape), whole(down.shape), ANYWHERE],
        out_specs=[whole(shape)] * 3,
        compiler_params=room(12),
        cost_estimate=cost(0, 6 * MIB),
        name="repack",
    )(up, down, after)


def join_kernel(picks, core_ref, *refs):
    count = len(picks)
    out_ref, mark_ref = refs[-2:]
    mark_ref[...] = jnp.zeros_like(mark_ref)
    for n, (_, *more) in enumerate(picks):
        place = slice(n * BLOCK, (n + 1) * BLOCK)
        value = refs[n][...]
        for add, at in more:
            value = value.astype(F32) + refs[count + add][at * BLOCK : (at + 1) * BLOCK].astype(F32)
        out_ref[place] = value.astype(BF)


def join(core, delta, picks, adds=(), after=()):
    half = delta.shape[1]
    shape = (len(picks) * BLOCK, half)

    def block(numbers):
        return pl.BlockSpec(
            (BLOCK, half), lambda i, c: (jnp.where(c[0] == 0, numbers[0], numbers[1]), 0)
        )

    return pl.pallas_call(
        lambda *refs: join_kernel(picks, *refs),
        out_shape=(jax.ShapeDtypeStruct(shape, BF), MARKED),
        grid_spec=pltpu.PrefetchScalarGridSpec(
            num_scalar_prefetch=1,
            grid=(1,),
            in_specs=[block(pick[0]) for pick in picks]
            + [whole(v.shape) for v in adds]
            + [whole(MARK)] * len(after),
            out_specs=(whole(shape), whole(MARK)),
        ),
        compiler_params=room(12),
        cost_estimate=cost(0, 4 * MIB),
        name="join",
    )(core, *([delta] * len(picks)), *adds, *after)


def piece_copy(piece, core, take, height, target, sem):
    if take is None:
        half = target.shape[1]
        piece = piece.at[:, pl.ds(pl.multiple_of(core * half, half), half)]
    else:
        piece = piece.at[pl.ds(take, height), :]
    return pltpu.make_async_copy(piece, target, sem)


def picked(refs, order_ref, numbers):
    return jnp.concatenate(
        [
            jnp.concatenate([ref[:, columns(order_ref, n)] for n in numbers], axis=1)
            for ref in refs
        ],
        axis=0,
    )


def begin_kernel(places, resid_places, order_ref, core_ref, weight_ref, *refs):
    count = len(places) + len(resid_places)
    pieces, refs = refs[:count], refs[count:]
    total_ref, rows_ref, turned_ref, mark_ref, held, resid, sems = refs[-7:]
    i = pl.program_id(0)
    tiles = pl.num_programs(0) // CORES
    copies, groups = [], []
    for n, (take, at, high) in enumerate(places + resid_places):
        target = held if n < len(places) else resid
        copies.append(
            piece_copy(pieces[n], core_ref[0], take, high, target.at[pl.ds(at, high), :], sems.at[n])
        )
        groups.append(at * CORES // target.shape[0])

    @pl.when(i == 0)
    def _():
        for e in range(CORES):
            for n, copy in enumerate(copies):
                if groups[n] == e:
                    copy.start()

    for e in range(CORES):

        @pl.when(i == e * tiles)
        def _():
            for n, copy in enumerate(copies):
                if groups[n] == e:
                    copy.wait()

    tile = held.at[pl.ds(pl.multiple_of(i * TALL_TILE, TALL_TILE), TALL_TILE), :]
    rows = tile[...]
    rows_ref[...] = rows
    turned_ref[...] = rows.T
    mark_ref[...] = jnp.zeros_like(mark_ref)
    value = dot(picked([tile], order_ref, range(SIDE)), weight_ref[...], NN)
    with_resid = resid.shape[0] // CORES // TALL_TILE
    inside = i % tiles

    @pl.when(inside < with_resid)
    def _():
        at = pl.multiple_of((i // tiles * with_resid + inside) * TALL_TILE, TALL_TILE)
        total_ref[...] = (value + resid[pl.ds(at, TALL_TILE), :].astype(F32)).astype(BF)

    @pl.when(inside >= with_resid)
    def _():
        total_ref[...] = value.astype(BF)


def begin(order, core, weight, pieces, places, resid_pieces, resid_places):
    height = sum(place[2] for place in places)
    depth = pieces[0].shape[1]
    half = weight.shape[1]
    tile = lambda width: pl.BlockSpec((TALL_TILE, width), lambda i: (i, 0))
    count = len(pieces) + len(resid_pieces)
    return pl.pallas_call(
        lambda *refs: begin_kernel(places, resid_places, *refs),
        out_shape=(
            jax.ShapeDtypeStruct((height, half), BF),
            jax.ShapeDtypeStruct((height, depth), BF),
            jax.ShapeDtypeStruct((depth, height), BF),
            MARKED,
        ),
        grid=(height // TALL_TILE,),
        in_specs=[SCALARS, SCALARS, whole(weight.shape)] + [ANYWHERE] * count,
        out_specs=(
            tile(half),
            tile(depth),
            pl.BlockSpec((depth, TALL_TILE), lambda i: (0, i)),
            whole(MARK),
        ),
        scratch_shapes=[
            pltpu.VMEM((height, depth), BF),
            pltpu.VMEM((sum(place[2] for place in resid_places), half), BF),
            pltpu.SemaphoreType.DMA((count,)),
        ],
        compiler_params=room(48),
        cost_estimate=cost(2 * height * weight.size, 30 * MIB),
        name="begin",
    )(order, core, weight, *pieces, *resid_pieces)


def contract_kernel(order_ref, total_ref, rows_ref, own_ref, got_ref, *refs):
    weights, refs = refs[: SIDE - 1], refs[SIDE - 1 :]
    out_ref, last_ref, turned_ref, weight, sems = refs
    i = pl.program_id(0)
    last = pl.num_programs(0) - 1
    block = SIDE * BLOCK
    loads = [
        pltpu.make_async_copy(part, weight.at[pl.ds((n + 2) % 3 * block, block), :], sems.at[n])
        for n, part in enumerate(weights)
    ]

    @pl.when(i == 0)
    def _():
        for n in (1, 2, 0):
            loads[n].start()
        for n in (1, 2):
            loads[n].wait()

    later = range(SIDE, 3 * SIDE)
    final = range(3 * SIDE, 4 * SIDE)

    @pl.when(i < last)
    def _():
        value = dot(picked([rows_ref], order_ref, later), weight[: 2 * block, :], NN)
        out_ref[...] = (total_ref[...].astype(F32) + value).astype(BF)
        last_ref[...] = picked([rows_ref], order_ref, final)

    @pl.when(i == last)
    def _():
        loads[0].wait()
        late = [own_ref, got_ref]
        left = picked(late, order_ref, [*later, *range(SIDE)])
        out_ref[...] = dot(left, weight[...], NN).astype(BF)
        turned_ref[:, :BLOCK] = own_ref[...].T
        turned_ref[:, BLOCK:] = got_ref[...].T
        last_ref[...] = picked(late, order_ref, final)


def contract(order, total, rows, late, parts):
    height, depth = rows.shape
    half = total.shape[1]
    end = height // TALL_TILE - 1
    kept = lambda width: pl.BlockSpec((TALL_TILE, width), lambda i: (jnp.minimum(i, end), 0))
    tile = lambda width: pl.BlockSpec((TALL_TILE, width), lambda i: (i, 0))
    return pl.pallas_call(
        contract_kernel,
        out_shape=(
            jax.ShapeDtypeStruct((height + TALL_TILE, half), BF),
            jax.ShapeDtypeStruct((height + TALL_TILE, SIDE * BLOCK), BF),
            jax.ShapeDtypeStruct((depth, TALL_TILE), BF),
        ),
        grid=(end + 2,),
        in_specs=[SCALARS, kept(half), kept(depth)]
        + [whole(v.shape) for v in late]
        + [ANYWHERE] * len(parts),
        out_specs=(tile(half), tile(SIDE * BLOCK), whole((depth, TALL_TILE))),
        scratch_shapes=[
            pltpu.VMEM((len(parts) * SIDE * BLOCK, half), BF),
            pltpu.SemaphoreType.DMA((len(parts),)),
        ],
        compiler_params=room(56),
        cost_estimate=cost(4 * height * parts[0].size, height * half * 8),
        name="contract",
    )(order, total, rows, *late, *parts)


def mix_kernel(places, own, total_ref, lefts_ref, *refs):
    count = len(places)
    weights, pieces, refs = refs[:2], refs[2 : 2 + count], refs[2 + count :]
    low_ref, raw_ref, square_ref, held, lows, weight, sems, weight_sems = refs
    i = pl.program_id(0)
    last = pl.num_programs(0) - 1
    tiles = last // CORES
    main = tiles * TALL_TILE
    copies = [
        piece_copy(pieces[n], 0, take, high, held.at[pl.ds(at, high), :], sems.at[n])
        for n, (take, at, high) in enumerate(places)
    ]
    high = weights[0].shape[0]
    loads = [
        pltpu.make_async_copy(part, weight.at[pl.ds(n * high, high), :], weight_sems.at[n])
        for n, part in enumerate(weights)
    ]

    @pl.when(i == 0)
    def _():
        for copy in loads + copies:
            copy.start()
        for load in loads:
            load.wait()

    def finish(resid):
        rows = pl.ds(pl.multiple_of(i * TALL_TILE, TALL_TILE), TALL_TILE)
        value = total_ref[...].astype(F32) + dot(lefts_ref[...], weight[...], NN)
        if resid is not None:
            value = value + resid.astype(F32)
        low = value.astype(BF)
        low_ref[...] = low
        lows[rows, :] = low
        squares = jnp.sum(value * value, axis=1, keepdims=True)
        square_ref[...] = jnp.broadcast_to(squares, square_ref.shape)

    plain = (i % tiles != tiles - 1) & (i != last)

    @pl.when(plain)
    def _():
        finish(None)

    @pl.when(jnp.logical_not(plain))
    def _():
        which = jnp.where(i == last, CORES, i // tiles)
        for e in range(3):

            @pl.when(which == e)
            def _():
                for n, place in enumerate(places):
                    if place[1] // TALL_TILE == e:
                        copies[n].wait()

        finish(held[pl.ds(pl.multiple_of(which * TALL_TILE, TALL_TILE), TALL_TILE), :])

    for e in range(CORES):
        base = e * main

        @pl.when(i == (e + 1) * tiles - 1)
        def _():
            raw_ref[e, : main - own] = dot(
                lows[base + own : base + main, :], lows[base : base + own, :], NT
            )

        @pl.when(i == last)
        def _():
            start = CORES * main + e * BLOCK
            raw_ref[e, main - own :] = dot(
                lows[start : start + BLOCK, :], lows[base : base + own, :], NT
            )


def mix(total, lefts, parts, pieces, places, own):
    height, half = total.shape
    tile = lambda width: pl.BlockSpec((TALL_TILE, width), lambda i: (i, 0))
    raw = (CORES, height // CORES - own, own)
    return pl.pallas_call(
        lambda *refs: mix_kernel(places, own, *refs),
        out_shape=(
            jax.ShapeDtypeStruct((height, half), BF),
            jax.ShapeDtypeStruct(raw, F32),
            jax.ShapeDtypeStruct((height, BLOCK), F32),
        ),
        grid=(height // TALL_TILE,),
        in_specs=[tile(half), tile(lefts.shape[1])] + [ANYWHERE] * (len(parts) + len(pieces)),
        out_specs=(tile(half), whole(raw), tile(BLOCK)),
        scratch_shapes=[
            pltpu.VMEM((3 * TALL_TILE, half), BF),
            pltpu.VMEM((height, half), BF),
            pltpu.VMEM((SIDE * BLOCK, half), BF),
            pltpu.SemaphoreType.DMA((len(pieces),)),
            pltpu.SemaphoreType.DMA((len(parts),)),
        ],
        compiler_params=room(56),
        cost_estimate=cost(2 * height * 512 * half, height * half * 10),
        name="mix",
    )(total, lefts, *parts, *pieces)


def project_kernel(low_ref, grad_q_ref, grad_p_ref, coef_ref, delta_ref):
    cores, queries, own = grad_q_ref.shape
    main = (low_ref.shape[0] - cores * BLOCK) // cores
    for e in range(cores):
        coef = coef_ref[e].T
        base, tail = e * main, cores * main + e * BLOCK
        low_p = low_ref[base : base + own]
        low_q = low_ref[base + own : base + main]
        low_t = low_ref[tail : tail + BLOCK]
        near = main - own
        up_p = dot(grad_p_ref[e], jnp.concatenate([low_q, low_t], axis=0), TN)
        up_q = dot(grad_q_ref[e], low_p, NN)
        delta_ref[base : base + own] = (
            up_p * coef[:own, 0:1] - low_p.astype(F32) * coef[:own, 1:2]
        ).astype(BF)
        delta_ref[base + own : base + main] = (
            up_q[:near] * coef[own:main, 0:1] - low_q.astype(F32) * coef[own:main, 1:2]
        ).astype(BF)
        delta_ref[tail : tail + BLOCK] = (
            up_q[near:] * coef[main:, 0:1] - low_t.astype(F32) * coef[main:, 1:2]
        ).astype(BF)


def project(low, grad_q, grad_p, coef):
    height, half = low.shape
    slab = half // 4
    block = pl.BlockSpec((height, slab), lambda h: (0, h))
    return pl.pallas_call(
        project_kernel,
        out_shape=jax.ShapeDtypeStruct(low.shape, BF),
        grid=(4,),
        in_specs=[block, whole(grad_q.shape), whole(grad_p.shape), whole(coef.shape)],
        out_specs=block,
        compiler_params=room(24),
        cost_estimate=cost(4 * grad_q.size * half, low.size * 4),
        name="project",
    )(low, grad_q, grad_p, coef)


def term_kernel(groups, added, order_ref, *refs):
    count = sum(len(picks) for picks in groups)
    lefts, rests, refs = refs[:count], refs[count : 2 * count], refs[2 * count :]
    delta_ref, adds = refs[0], refs[1 : 1 + added]
    outs, (mark_ref, left) = refs[-2 - len(groups) : -2], refs[-2:]
    mark_ref[...] = jnp.zeros_like(mark_ref)
    main = lefts[0].shape[1]

    @pl.when(pl.program_id(0) == 0)
    def _():
        for k in range(count):
            left[k * BLOCK : (k + 1) * BLOCK, :main] = lefts[k][...]
            left[k * BLOCK : (k + 1) * BLOCK, main:] = rests[k][...]

    value = dot(left[...], delta_ref[...], NN)
    at = 0
    for n, out_ref in enumerate(outs):
        height = out_ref.shape[0]
        part = value[at : at + height]
        if added:
            part = part + adds[n][...].astype(F32)
        out_ref[...] = part.astype(BF)
        at += height


def term(order, turned, delta, groups, adds=(), after=()):
    height, half = delta.shape
    slab = half // 4
    picks = [n for group in groups for n in group]
    lefts = [
        pl.BlockSpec(
            (BLOCK, v.shape[1]), lambda i, o, n=n: (o[n], 0), pipeline_mode=pl.Buffered(1)
        )
        for v in turned
        for n in picks
    ]
    sizes = [len(group) * BLOCK for group in groups]
    count = len(picks)
    return pl.pallas_call(
        lambda *refs: term_kernel(groups, len(adds), *refs),
        out_shape=[jax.ShapeDtypeStruct((size, half), BF) for size in sizes] + [MARKED],
        grid_spec=pltpu.PrefetchScalarGridSpec(
            num_scalar_prefetch=1,
            grid=(4,),
            in_specs=lefts
            + [pl.BlockSpec((height, slab), lambda i, o: (0, i))]
            + [pl.BlockSpec((v.shape[0], slab), lambda i, o: (0, i)) for v in adds]
            + [whole(MARK)] * len(after),
            out_specs=[pl.BlockSpec((size, slab), lambda i, o: (0, i)) for size in sizes]
            + [whole(MARK)],
            scratch_shapes=[pltpu.VMEM((count * BLOCK, height), BF)],
        ),
        compiler_params=room(24),
        cost_estimate=cost(2 * height * count * BLOCK * half, height * (half + 512) * 2),
        name="term",
    )(order, *([turned[0]] * count), *([turned[1]] * count), delta, *adds, *after)


def settle_kernel(own_ref, *refs):
    refs[-1][...] = jnp.zeros_like(refs[-1])
    for n in range(2):
        one, two = refs[2 * n], refs[2 * n + 1]
        height = one.shape[0]
        value = own_ref[n * height : (n + 1) * height].astype(F32)
        value = value + one[...].astype(F32) + two[...].astype(F32)
        for k in range(2):
            refs[-SIDE - 1 + 2 * n + k][...] = value[k * BLOCK : (k + 1) * BLOCK].astype(BF)


def settle(own, tops, bottoms, after):
    height, half = own.shape
    slab = half // 4
    part = pl.BlockSpec((height // 2, slab), lambda i: (0, i))
    return pl.pallas_call(
        settle_kernel,
        out_shape=[jax.ShapeDtypeStruct((BLOCK, half), BF)] * SIDE + [MARKED],
        grid=(4,),
        in_specs=[pl.BlockSpec((height, slab), lambda i: (0, i))]
        + [part] * 4
        + [whole(MARK)] * len(after),
        out_specs=[pl.BlockSpec((BLOCK, slab), lambda i: (0, i))] * SIDE + [whole(MARK)],
        compiler_params=room(16),
        cost_estimate=cost(0, 8 * MIB),
        name="settle",
    )(own, *tops, *bottoms, *after)


def gather_kernel(*refs):
    value = refs[0][...].astype(F32)
    for ref in refs[1:SIDE]:
        value = value + ref[...].astype(F32)
    refs[-1][...] = value.astype(BF)


def gather(blocks, after):
    height, half = blocks[0].shape
    tile = pl.BlockSpec((height, half // 2), lambda i: (0, i))
    return pl.pallas_call(
        gather_kernel,
        out_shape=jax.ShapeDtypeStruct((height, half), BF),
        grid=(2,),
        in_specs=[tile] * SIDE + [whole(MARK)],
        out_specs=tile,
        compiler_params=room(12),
        cost_estimate=cost(0, 4 * MIB),
        name="gather",
    )(*blocks, after)


def back_kernel(order_ref, own_rows_ref, other_rows_ref, *refs):
    weights, (own_ref, other_ref, mark_ref, held, sems) = refs[: SIDE + 1], refs[-5:]
    mark_ref[...] = jnp.zeros_like(mark_ref)
    copies, at = [], 0
    for n, weight in enumerate(weights):
        height = weight.shape[0]
        copies.append(
            pltpu.make_async_copy(weight, held.at[pl.ds(at, height), :], sems.at[n])
        )
        copies[-1].start()
        at += height
    at = 0
    rows = own_ref.shape[0]
    left = jnp.concatenate([own_rows_ref[...], other_rows_ref[...]], axis=0)
    for n, weight in enumerate(weights):
        height = weight.shape[0]
        copies[n].wait()
        value = dot(left, held[at : at + height, :], NT)
        for k in range(height // BLOCK):
            place = columns(order_ref, at // BLOCK + k)
            piece = value[:, k * BLOCK : (k + 1) * BLOCK]
            own_ref[:, place] = piece[:rows]
            other_ref[:, place] = piece[rows:].astype(BF)
        at += height


def back(order, delta, height, places, parts, after):
    half = delta.shape[1]
    depth = sum(part.shape[0] for part in parts)
    return pl.pallas_call(
        back_kernel,
        out_shape=(
            jax.ShapeDtypeStruct((height, depth), F32),
            jax.ShapeDtypeStruct((height, depth), BF),
            MARKED,
        ),
        grid=(1,),
        in_specs=[SCALARS]
        + [pl.BlockSpec((height, half), lambda i, n=n: (n // height, 0)) for n in places]
        + [ANYWHERE] * len(parts)
        + [whole(MARK)] * len(after),
        out_specs=(whole((height, depth)), whole((height, depth)), whole(MARK)),
        scratch_shapes=[
            pltpu.VMEM((depth, half), BF),
            pltpu.SemaphoreType.DMA((len(parts),)),
        ],
        compiler_params=room(28),
        cost_estimate=cost(4 * height * depth * half, 14 * MIB),
        name="back",
    )(order, delta, delta, *parts, *after)


def lay_kernel(core_ref, own_ref, got_ref, out_ref):
    i = pl.program_id(0)

    @pl.when(i < 2)
    def _():
        out_ref[...] = own_ref[...]

    @pl.when(i >= 2)
    def _():
        out_ref[...] = got_ref[...]


def lay(core, delta, got):
    height, half = got.shape
    quarter = half // 2
    return pl.pallas_call(
        lay_kernel,
        out_shape=jax.ShapeDtypeStruct((height, 4 * quarter), BF),
        grid_spec=pltpu.PrefetchScalarGridSpec(
            num_scalar_prefetch=1,
            grid=(4,),
            in_specs=[
                pl.BlockSpec((height, quarter), lambda i, core: (0, jnp.minimum(i, 1))),
                pl.BlockSpec((height, quarter), lambda i, core: (0, jnp.maximum(i - 2, 0))),
            ],
            out_specs=pl.BlockSpec(
                (height, quarter),
                lambda i, core: (0, jnp.where(i < 2, 2 * core[0], 2 * (1 - core[0]) - 2) + i),
            ),
        ),
        compiler_params=room(12),
        cost_estimate=cost(0, 16 * height * quarter),
        name="lay",
    )(core, delta, got)


def body(query_attn, query_resid, passage_attn, passage_resid, out_weight, hard_lists, positive):
    z = lax.axis_index("dp")
    f = lax.axis_index("fsdp")
    c, x, y = f % CORES, (f // CORES) % SIDE, f // (SIDE * CORES)
    first = c == 0
    width = query_resid.shape[1]
    half = width // 2
    own_rows = passage_attn.shape[0]
    blocks = own_rows // BLOCK

    core = c.astype(jnp.int32).reshape(1)

    got = swap(other_halves(core, [out_weight, query_resid]))
    shard = chip_shard(core, out_weight, got)
    near = [shard, first_up(shard), first_down(shard), first_across(shard)]
    hops = jnp.array(HOPS, jnp.int32)
    ys, xs = (y + hops) % SIDE, (x + hops) % SIDE
    order = jnp.where(
        first, ys[:, None] * SIDE + xs[None, :], ys[None, :] * SIDE + xs[:, None]
    )
    order = order.reshape(-1).astype(jnp.int32)

    attn_up, attn_down = z_up(query_attn), z_down(query_attn)
    resid = pair_rows(core, query_resid, got)
    numbers = jnp.concatenate([hard_lists.reshape(-1), positive])
    other_numbers = swap(numbers)
    weight, to_up, to_down, three = pack(near, query_attn, attn_up, attn_down, resid)
    parts = [weight, second_up(weight), second_down(weight)]
    from_up, from_down = z_up(to_up), z_down(to_down)
    pieces = [passage_attn, three, swap(passage_attn), swap(three)]
    main = own_rows + 3 * BLOCK
    places = [
        (0, 0, own_rows),
        (0, own_rows, 3 * BLOCK),
        (0, main, own_rows),
        (0, main + own_rows, 3 * BLOCK),
    ]
    span = own_rows + BLOCK
    other_resid = swap(other_half(core, passage_resid))
    resid_pieces = [passage_resid, resid, other_resid, resid]
    resid_places = [
        (None, 0, own_rows),
        (0, own_rows, BLOCK),
        (0, span, own_rows),
        (BLOCK, span + own_rows, BLOCK),
    ]
    total, rows, turned, mark = begin(
        order, core, weight, pieces, places, resid_pieces, resid_places
    )
    on_up, on_down = halves(parts[1], parts[2], [mark])
    parts += [second_up(on_up), second_down(on_down)]
    resid_up, resid_down, attn_far = repack(from_up, from_down, other_numbers)
    far_up, far_down = z_up(resid_up), z_down(resid_down)
    late = [attn_far, swap(attn_far)]

    total, lefts, turned_far = contract(order, total, rows, late, parts[:3])
    turned = (turned, turned_far)
    part = BLOCK // 2
    pieces = [from_up, from_down, from_up, from_down, far_up, far_down]
    places = [(part + n // 2 * BLOCK, n * BLOCK, BLOCK) for n in range(4)]
    places += [(0, n * BLOCK, BLOCK) for n in (4, 5)]
    low, raw, squares = mix(total, lefts, parts[3:], pieces, places, own_rows)
    squares = squares[:, 0]
    raw = raw.reshape(CORES, SIDE, BLOCK, own_rows)

    squares = squares + jnp.concatenate(
        [squares_in for squares_in in (lambda v: (
            v[main : 2 * main], v[:main], v[2 * main + BLOCK :], v[2 * main : 2 * main + BLOCK]
        ))(swap(squares))]
    )
    squares = jnp.concatenate(
        [squares[: CORES * main].reshape(CORES, main), squares[CORES * main :].reshape(CORES, BLOCK)],
        axis=1,
    )
    squares_p = squares[:, :own_rows]
    squares_q = squares[:, own_rows:].reshape(CORES, SIDE, BLOCK)
    raw = raw + swap(raw)[::-1]
    factor_p = lax.rsqrt(squares_p + epsilon)
    factor_q = lax.rsqrt(squares_q + epsilon)

    listed = hard_lists.size
    lists = jnp.stack([numbers[:listed], other_numbers[:listed]]).reshape(CORES, SIDE, -1)
    ks = jnp.arange(SIDE, dtype=jnp.int32)
    source = (z + hops) % SIDE
    asked = jnp.take(lists, source, axis=1)
    ids = z * blocks + jnp.arange(blocks, dtype=jnp.int32)
    wanted = jnp.any(asked[:, :, :, None] == ids, axis=2)
    wanted = wanted | (ks == 0)[None, :, None]
    wanted = jnp.repeat(wanted, BLOCK, axis=2)[:, :, None, :]
    hits = jnp.stack([numbers[listed:], other_numbers[listed:]])
    target = (jnp.arange(own_rows, dtype=jnp.int32) == hits[:, :, None])[:, None]
    target = (target & (ks == 0)[None, :, None, None]).astype(F32)

    scores = sharpness * raw * factor_q[..., None] * factor_p[:, None, None, :]
    scores = jnp.where(wanted, scores, -1e30)
    highest = jnp.max(scores, axis=3)
    totals = jnp.sum(jnp.exp(scores - highest[..., None]), axis=3)
    stats = jnp.stack([highest, totals])
    all_stats = [stats]
    for k in range(1, SIDE):
        got = z_to[-HOPS[k] % SIDE](stats)
        picks = [[h % SIDE for h in HOPS].index((h - HOPS[k]) % SIDE) for h in HOPS]
        all_stats.append(jnp.concatenate([got[:, :, i : i + 1] for i in picks], axis=2))
    top = all_stats[0][0]
    for v in all_stats[1:]:
        top = jnp.maximum(top, v[0])
    log_total = top + jnp.log(sum(v[1] * jnp.exp(v[0] - top) for v in all_stats))
    query_loss = log_total[0, 0] - jnp.sum(scores[0, 0] * target[0, 0], axis=1)

    scale = sharpness / (BLOCK * DEVICES)
    grad = scale * (jnp.exp(scores - log_total[..., None]) - target)
    weighted = grad * scores * (1.0 / sharpness)
    inner_q = jnp.sum(weighted, axis=3)
    inner_p = jnp.sum(weighted, axis=(1, 2))
    grad_q = (grad * factor_p[:, None, None, :]).astype(BF).reshape(CORES, -1, own_rows)
    grad_p = (grad * factor_q[..., None]).astype(BF).reshape(CORES, -1, own_rows)
    factors = jnp.concatenate([factor_p, factor_q.reshape(CORES, -1)], axis=1)
    inners = jnp.concatenate([inner_p, inner_q.reshape(CORES, -1)], axis=1)
    coef = jnp.stack([factors, factors * factors * inners], axis=1)
    delta = project(low, grad_q, grad_p, coef)

    def at(e, j):
        return (e * main + own_rows) // BLOCK + j

    def both(e, j, k):
        return at(e, j), at(e, k)

    end = CORES * main // BLOCK
    far_top, far_bottom, mark = term(order, turned, delta, ((12, 13), (14, 15)))
    up, down = second_up(far_top), second_down(far_bottom)
    far, _ = join(core, delta, [((end + e,) * 2,) for e in range(CORES)], after=[mark])
    far = z_with(far)
    up_bottom, down_top, mark = term(
        order, turned, delta, ((10, 11), (4, 5)), after=[mark]
    )
    got_bottom, got_top = second_up(up_bottom), second_down(down_top)
    up_top, down_bottom, mark = term(
        order, turned, delta, ((8, 9), (6, 7)), [up, down], [mark]
    )
    got_tops = [got_top, second_up(up_top)]
    got_bottoms = [got_bottom, second_down(down_bottom)]
    own_sum, mark = term(order, turned, delta, ((0, 1, 2, 3),), after=[mark])
    flow, mark = join(
        core, delta, [(both(e, 2, 1), (0, e)) for e in range(CORES)], [far], [mark]
    )
    counter, counter_mark = join(
        core, delta, [(both(e, 1, 2),) for e in range(CORES)], after=[mark]
    )
    z_got = [z_with(flow), z_against(counter)]
    *sums, mark = settle(own_sum, got_tops, got_bottoms, [mark, counter_mark])
    *passage_parts, back_mark = back(order, delta, own_rows, (0, main), parts, [mark])
    theirs, _ = join(
        core,
        delta,
        [(both(1, k, k),) for k in range(-own_rows // BLOCK, 0)],
        after=[back_mark],
    )
    summed, _ = join(
        core, delta, [(both(e, 0, 0), (0, e), (1, e)) for e in range(CORES)], z_got, [back_mark]
    )
    got = [sums[0], first_down(sums[1]), first_up(sums[2]), first_across(sums[3])]
    part = gather(got, back_mark)
    part = part.reshape(CORES, SIDE, BLOCK // 8, half)

    def pick(v, index, axis):
        return lax.dynamic_index_in_dim(v, index, axis, keepdims=False)

    total = pick(part, z, 1).astype(F32)
    for k in (1, 3, 2):
        total = total + z_to[k](pick(part, (z + k) % SIDE, 1)).astype(F32)
    total = total.astype(BF)
    own, other = pick(total, c, 0), swap(pick(total, 1 - c, 0))
    total = jnp.where(
        first, jnp.concatenate([own, other], axis=1), jnp.concatenate([other, own], axis=1)
    )
    late_mark = total[: MARK[0], : MARK[1]].astype(F32)
    weight_grad = jnp.zeros((SIDE,) + total.shape, F32)
    for k in (0, 1, 3, 2):
        got = total if k == 0 else z_to[k](total)
        weight_grad = lax.dynamic_update_index_in_dim(
            weight_grad, got.astype(F32), (z - k) % SIDE, 0
        )
    weight_grad = weight_grad.reshape(out_weight.shape)

    def finish(products, rows, theirs):
        own, other = products
        value = (own + swap(other).astype(F32)).astype(BF)
        return value, lay(core, rows, swap(theirs))

    passage_back, passage_delta = finish(passage_parts, delta, theirs)
    *query_parts, _ = back(order, summed, BLOCK, (0, BLOCK), parts, [late_mark])
    query_back, query_delta = finish(query_parts, summed, summed[BLOCK:])
    return (query_loss, query_back, query_delta, passage_back, passage_delta, weight_grad)


def solution(mesh):
    rows = P(("dp", "fsdp"), None)
    return jax.shard_map(
        body,
        mesh=mesh,
        in_specs=(
            rows,
            rows,
            rows,
            rows,
            P("fsdp", None),
            P("fsdp", None, None),
            P(("dp", "fsdp")),
        ),
        out_specs=(P(("dp", "fsdp")), rows, rows, rows, rows, P("fsdp", None)),
        check_vma=False,
    )
```

```python
import jax
import jax.numpy as jnp
from jax import lax
from jax.experimental import pallas as pl
from jax.experimental.pallas import tpu as pltpu
from jax.sharding import PartitionSpec as P

BLOCK = 128
SIDE = 4
CORES = 2
FSDP = SIDE * SIDE * CORES
DEVICES = SIDE * FSDP

sharpness = 250.0
epsilon = 1e-06
BF = jnp.bfloat16
F32 = jnp.float32


def route(target):
    pairs = []
    for source in range(DEVICES):
        z, rest = divmod(source, FSDP)
        y, rest = divmod(rest, SIDE * CORES)
        x, c = divmod(rest, CORES)
        z, y, x, c = target(z, y, x, c)
        pairs.append((source, (((z % SIDE) * SIDE + y % SIDE) * SIDE + x % SIDE) * CORES + c))
    return lambda value: lax.ppermute(value, ("dp", "fsdp"), pairs)


def way(c):
    return 1 - 2 * c


def along_first(shift):
    return route(
        lambda z, y, x, c: (z, y, x + shift, c) if c == 0 else (z, y + shift, x, c)
    )


def along_second(shift):
    return route(
        lambda z, y, x, c: (z, y + shift, x, c) if c == 0 else (z, y, x + shift, c)
    )


swap = route(lambda z, y, x, c: (z, y, x, 1 - c))
z_to = [route(lambda z, y, x, c, k=k: (z + k, y, x, c)) for k in range(SIDE)]
z_up, z_across, z_down = z_to[1:]
z_with = route(lambda z, y, x, c: (z + way(c), y, x, c))
z_against = route(lambda z, y, x, c: (z - way(c), y, x, c))
first_up, first_down, first_across = (along_first(shift) for shift in (1, -1, 2))
second_up, second_down = (along_second(shift) for shift in (1, -1))


def dot(a, b, dims, batch=((), ())):
    return lax.dot_general(a, b, (dims, batch), preferred_element_type=F32)


TALL_TILE = 256
MIB = 1024 * 1024
HOPS = (0, -1, 1, 2)
ANYWHERE = pl.BlockSpec(memory_space=pl.ANY)
SCALARS = pl.BlockSpec(memory_space=pltpu.SMEM)
NT = ((1,), (1,))
NN = ((1,), (0,))
TN = ((0,), (0,))


def cost(flops, traffic):
    return pl.CostEstimate(
        flops=int(flops) // 4, bytes_accessed=int(traffic) // 4, transcendentals=0
    )


def room(mib):
    return pltpu.CompilerParams(vmem_limit_bytes=mib * MIB)


def whole(shape):
    return pl.BlockSpec(shape, lambda *_: (0,) * len(shape), pipeline_mode=pl.Buffered(1))


MARK = (8, BLOCK)
MARKED = jax.ShapeDtypeStruct(MARK, F32)


def copy_kernel(core_ref, in_ref, *refs):
    refs[-1][...] = in_ref[...]


def other_half(core, rows, after=()):
    height, half = rows.shape[0], rows.shape[1] // 2
    return pl.pallas_call(
        copy_kernel,
        out_shape=jax.ShapeDtypeStruct((height, half), rows.dtype),
        grid_spec=pltpu.PrefetchScalarGridSpec(
            num_scalar_prefetch=1,
            grid=(1,),
            in_specs=[pl.BlockSpec((height, half), lambda i, core: (0, 1 - core[0]))]
            + [ANYWHERE] * len(after),
            out_specs=pl.BlockSpec((height, half), lambda i, core: (0, 0)),
        ),
        compiler_params=room(12),
        cost_estimate=cost(0, 4 * height * half),
        name="other_half",
    )(core, rows, *after)


def halves_of_kernel(core_ref, *refs):
    at = 0
    for ref in refs[:-1]:
        refs[-1][at : at + ref.shape[0]] = ref[...]
        at += ref.shape[0]


def other_halves(core, arrays):
    half = arrays[0].shape[1] // 2
    shape = (sum(v.shape[0] for v in arrays), half)
    return pl.pallas_call(
        halves_of_kernel,
        out_shape=jax.ShapeDtypeStruct(shape, BF),
        grid_spec=pltpu.PrefetchScalarGridSpec(
            num_scalar_prefetch=1,
            grid=(1,),
            in_specs=[
                pl.BlockSpec((v.shape[0], half), lambda i, core: (0, 1 - core[0])) for v in arrays
            ],
            out_specs=whole(shape),
        ),
        compiler_params=room(8),
        cost_estimate=cost(0, 4 * shape[0] * half),
        name="other_halves",
    )(core, *arrays)


def shard_kernel(core_ref, own_ref, got_ref, out_ref):
    core = core_ref[0]
    height = own_ref.shape[0]
    for rows, at in ((own_ref, core), (got_ref, 1 - core)):
        out_ref[pl.ds(pl.multiple_of(at * height, height), height), :] = rows[:height]


def chip_shard(core, weight, got):
    height, half = weight.shape[0], got.shape[1]
    return pl.pallas_call(
        shard_kernel,
        out_shape=jax.ShapeDtypeStruct((CORES * height, half), weight.dtype),
        grid_spec=pltpu.PrefetchScalarGridSpec(
            num_scalar_prefetch=1,
            grid=(1,),
            in_specs=[
                pl.BlockSpec((height, half), lambda i, core: (0, core[0])),
                whole(got.shape),
            ],
            out_specs=whole((CORES * height, half)),
        ),
        compiler_params=room(12),
        cost_estimate=cost(0, 8 * height * half),
        name="chip_shard",
    )(core, weight, got)


def pair_rows_kernel(core_ref, own_ref, got_ref, out_ref):
    height = own_ref.shape[0]
    out_ref[:height] = own_ref[...]
    out_ref[height:] = got_ref[got_ref.shape[0] - height :]


def pair_rows(core, rows, got):
    height, half = rows.shape[0], got.shape[1]
    return pl.pallas_call(
        pair_rows_kernel,
        out_shape=jax.ShapeDtypeStruct((CORES * height, half), rows.dtype),
        grid_spec=pltpu.PrefetchScalarGridSpec(
            num_scalar_prefetch=1,
            grid=(1,),
            in_specs=[pl.BlockSpec((height, half), lambda i, core: (0, core[0])), whole(got.shape)],
            out_specs=whole((CORES * height, half)),
        ),
        compiler_params=room(12),
        cost_estimate=cost(0, 8 * height * half),
        name="pair_rows",
    )(core, rows, got)


def columns(order_ref, i):
    return pl.ds(pl.multiple_of(order_ref[i] * BLOCK, BLOCK), BLOCK)


def lead_kernel(core_ref, attn_ref, resid_ref, out_ref):
    out_ref[:BLOCK] = attn_ref[...]
    out_ref[BLOCK:] = resid_ref[...]


def lead(core, attn, resid):
    shape = (2 * BLOCK, attn.shape[1])
    return pl.pallas_call(
        lead_kernel,
        out_shape=jax.ShapeDtypeStruct(shape, BF),
        grid_spec=pltpu.PrefetchScalarGridSpec(
            num_scalar_prefetch=1,
            grid=(1,),
            in_specs=[
                whole(attn.shape),
                pl.BlockSpec(attn.shape, lambda i, core: (0, core[0])),
            ],
            out_specs=whole(shape),
        ),
        compiler_params=room(8),
        cost_estimate=cost(0, 2 * MIB),
        name="lead",
    )(core, attn, resid)


def pack_kernel(attn_ref, up_ref, down_ref, resid_ref, to_up, to_down, three_ref):
    part = BLOCK // 2
    to_up[:part] = up_ref[:part]
    to_up[part:] = resid_ref[...]
    to_down[:part] = down_ref[part:BLOCK]
    to_down[part:] = resid_ref[...]
    for n, row in enumerate((attn_ref, up_ref, down_ref)):
        three_ref[n * BLOCK : (n + 1) * BLOCK] = row[:BLOCK]


def pack(attn, up, down, resid):
    half = attn.shape[1]
    shapes = [(BLOCK // 2 + BLOCK, half)] * 2 + [(3 * BLOCK, half)]
    operands = [attn, up, down]
    last = resid.shape[0] // BLOCK - 1
    return pl.pallas_call(
        pack_kernel,
        out_shape=[jax.ShapeDtypeStruct(s, BF) for s in shapes],
        grid=(1,),
        in_specs=[whole(v.shape) for v in operands]
        + [pl.BlockSpec((BLOCK, half), lambda i: (last, 0))],
        out_specs=[whole(s) for s in shapes],
        compiler_params=room(56),
        cost_estimate=cost(0, 8 * MIB),
        name="pack",
    )(*operands, resid)


def stack_kernel(*refs):
    out_ref = refs[-1]
    for n, row in enumerate(refs[:-1]):
        out_ref[n * BLOCK : (n + 1) * BLOCK] = row[...]


def stack(blocks):
    half = blocks[0].shape[1]
    shape = (len(blocks) * BLOCK, half)
    return pl.pallas_call(
        stack_kernel,
        out_shape=jax.ShapeDtypeStruct(shape, BF),
        grid=(1,),
        in_specs=[whole(v.shape) for v in blocks],
        out_specs=whole(shape),
        compiler_params=room(16),
        cost_estimate=cost(0, 4 * MIB),
        name="stack",
    )(*blocks)


def halves_kernel(one_ref, two_ref, *refs):
    refs[-2][...] = one_ref[...]
    refs[-1][...] = two_ref[...]


def halves(one, two, after):
    height, half = one.shape
    shape = (height // 2, half)
    return pl.pallas_call(
        halves_kernel,
        out_shape=[jax.ShapeDtypeStruct(shape, BF)] * 2,
        grid=(1,),
        in_specs=[
            pl.BlockSpec(shape, lambda i: (0, 0)),
            pl.BlockSpec(shape, lambda i: (1, 0)),
        ]
        + [whole(MARK)] * len(after),
        out_specs=[whole(shape)] * 2,
        compiler_params=room(16),
        cost_estimate=cost(0, 8 * MIB),
        name="halves",
    )(one, two, *after)


def repack_kernel(near_ref, up_ref, down_ref, *refs):
    outs = refs[-3:]
    part = BLOCK // 2
    outs[0][...] = near_ref[...]
    outs[1][...] = down_ref[part:]
    outs[2][:part] = up_ref[:part]
    outs[2][part:] = down_ref[:part]


def repack(near, up, down, after):
    shape = (BLOCK, up.shape[1])
    return pl.pallas_call(
        repack_kernel,
        out_shape=[jax.ShapeDtypeStruct(shape, BF)] * 3,
        grid=(1,),
        in_specs=[
            pl.BlockSpec(shape, lambda i: (1, 0)),
            whole(up.shape),
            whole(down.shape),
            ANYWHERE,
        ],
        out_specs=[whole(shape)] * 3,
        compiler_params=room(12),
        cost_estimate=cost(0, 6 * MIB),
        name="repack",
    )(near, up, down, after)


def join_kernel(picks, core_ref, *refs):
    count = len(picks)
    out_ref, mark_ref = refs[-2:]
    mark_ref[...] = jnp.zeros_like(mark_ref)
    for n, (_, *more) in enumerate(picks):
        place = slice(n * BLOCK, (n + 1) * BLOCK)
        value = refs[n][...]
        for add, at in more:
            value = value.astype(F32) + refs[count + add][at * BLOCK : (at + 1) * BLOCK].astype(F32)
        out_ref[place] = value.astype(BF)


def join(core, delta, picks, adds=(), after=()):
    half = delta.shape[1]
    shape = (len(picks) * BLOCK, half)

    def block(numbers):
        return pl.BlockSpec(
            (BLOCK, half), lambda i, c: (jnp.where(c[0] == 0, numbers[0], numbers[1]), 0)
        )

    return pl.pallas_call(
        lambda *refs: join_kernel(picks, *refs),
        out_shape=(jax.ShapeDtypeStruct(shape, BF), MARKED),
        grid_spec=pltpu.PrefetchScalarGridSpec(
            num_scalar_prefetch=1,
            grid=(1,),
            in_specs=[block(pick[0]) for pick in picks]
            + [whole(v.shape) for v in adds]
            + [whole(MARK)] * len(after),
            out_specs=(whole(shape), whole(MARK)),
        ),
        compiler_params=room(20),
        cost_estimate=cost(0, 4 * MIB),
        name="join",
    )(core, *([delta] * len(picks)), *adds, *after)


def piece_copy(piece, core, take, height, target, sem):
    if take is None:
        half = target.shape[1]
        piece = piece.at[:, pl.ds(pl.multiple_of(core * half, half), half)]
    else:
        piece = piece.at[pl.ds(take, height), :]
    return pltpu.make_async_copy(piece, target, sem)


def picked(refs, order_ref, numbers):
    return jnp.concatenate(
        [
            jnp.concatenate([ref[:, columns(order_ref, n)] for n in numbers], axis=1)
            for ref in refs
        ],
        axis=0,
    )


def begin_kernel(places, resid_places, order_ref, core_ref, weight_ref, *refs):
    count = len(places) + len(resid_places)
    pieces, refs = refs[:count], refs[count:]
    total_ref, rows_ref, turned_ref, mark_ref, held, resid, sems = refs[-7:]
    i = pl.program_id(0)
    tiles = pl.num_programs(0) // CORES
    copies, groups = [], []
    for n, (take, at, high) in enumerate(places + resid_places):
        target = held if n < len(places) else resid
        copies.append(
            piece_copy(pieces[n], core_ref[0], take, high, target.at[pl.ds(at, high), :], sems.at[n])
        )
        groups.append(at * CORES // target.shape[0])

    @pl.when(i == 0)
    def _():
        for e in range(CORES):
            for n, copy in enumerate(copies):
                if groups[n] == e:
                    copy.start()

    for e in range(CORES):

        @pl.when(i == e * tiles)
        def _():
            for n, copy in enumerate(copies):
                if groups[n] == e:
                    copy.wait()

    tile = held.at[pl.ds(pl.multiple_of(i * TALL_TILE, TALL_TILE), TALL_TILE), :]
    rows = tile[...]
    rows_ref[...] = rows
    turned_ref[...] = rows.T
    mark_ref[...] = jnp.zeros_like(mark_ref)
    value = dot(picked([tile], order_ref, range(SIDE)), weight_ref[...], NN)
    with_resid = resid.shape[0] // CORES // TALL_TILE
    inside = i % tiles

    @pl.when(inside < with_resid)
    def _():
        at = pl.multiple_of((i // tiles * with_resid + inside) * TALL_TILE, TALL_TILE)
        total_ref[...] = (value + resid[pl.ds(at, TALL_TILE), :].astype(F32)).astype(BF)

    @pl.when(inside >= with_resid)
    def _():
        total_ref[...] = value.astype(BF)


def begin(order, core, weight, pieces, places, resid_pieces, resid_places):
    height = sum(place[2] for place in places)
    depth = pieces[0].shape[1]
    half = weight.shape[1]
    tile = lambda width: pl.BlockSpec((TALL_TILE, width), lambda i: (i, 0))
    count = len(pieces) + len(resid_pieces)
    return pl.pallas_call(
        lambda *refs: begin_kernel(places, resid_places, *refs),
        out_shape=(
            jax.ShapeDtypeStruct((height, half), BF),
            jax.ShapeDtypeStruct((height, depth), BF),
            jax.ShapeDtypeStruct((depth, height), BF),
            MARKED,
        ),
        grid=(height // TALL_TILE,),
        in_specs=[SCALARS, SCALARS, whole(weight.shape)] + [ANYWHERE] * count,
        out_specs=(
            tile(half),
            tile(depth),
            pl.BlockSpec((depth, TALL_TILE), lambda i: (0, i)),
            whole(MARK),
        ),
        scratch_shapes=[
            pltpu.VMEM((height, depth), BF),
            pltpu.VMEM((sum(place[2] for place in resid_places), half), BF),
            pltpu.SemaphoreType.DMA((count,)),
        ],
        compiler_params=room(48),
        cost_estimate=cost(2 * height * weight.size, 30 * MIB),
        name="begin",
    )(order, core, weight, *pieces, *resid_pieces)


def contract_kernel(order_ref, total_ref, rows_ref, own_ref, got_ref, *refs):
    weights, refs = refs[: SIDE - 1], refs[SIDE - 1 :]
    out_ref, last_ref, turned_ref, weight, sems = refs
    i = pl.program_id(0)
    last = pl.num_programs(0) - 1
    block = SIDE * BLOCK
    loads = [
        pltpu.make_async_copy(part, weight.at[pl.ds((n + 2) % 3 * block, block), :], sems.at[n])
        for n, part in enumerate(weights)
    ]

    @pl.when(i == 0)
    def _():
        for n in (1, 2, 0):
            loads[n].start()
        for n in (1, 2):
            loads[n].wait()

    later = range(SIDE, 3 * SIDE)
    final = range(3 * SIDE, 4 * SIDE)

    @pl.when(i < last)
    def _():
        value = dot(picked([rows_ref], order_ref, later), weight[: 2 * block, :], NN)
        out_ref[...] = (total_ref[...].astype(F32) + value).astype(BF)
        last_ref[...] = picked([rows_ref], order_ref, final)

    @pl.when(i == last)
    def _():
        loads[0].wait()
        late = [own_ref, got_ref]
        left = picked(late, order_ref, [*later, *range(SIDE)])
        out_ref[...] = dot(left, weight[...], NN).astype(BF)
        turned_ref[:, :BLOCK] = own_ref[...].T
        turned_ref[:, BLOCK:] = got_ref[...].T
        last_ref[...] = picked(late, order_ref, final)


def contract(order, total, rows, late, parts):
    height, depth = rows.shape
    half = total.shape[1]
    end = height // TALL_TILE - 1
    kept = lambda width: pl.BlockSpec((TALL_TILE, width), lambda i: (jnp.minimum(i, end), 0))
    tile = lambda width: pl.BlockSpec((TALL_TILE, width), lambda i: (i, 0))
    return pl.pallas_call(
        contract_kernel,
        out_shape=(
            jax.ShapeDtypeStruct((height + TALL_TILE, half), BF),
            jax.ShapeDtypeStruct((height + TALL_TILE, SIDE * BLOCK), BF),
            jax.ShapeDtypeStruct((depth, TALL_TILE), BF),
        ),
        grid=(end + 2,),
        in_specs=[SCALARS, kept(half), kept(depth)]
        + [whole(v.shape) for v in late]
        + [ANYWHERE] * len(parts),
        out_specs=(tile(half), tile(SIDE * BLOCK), whole((depth, TALL_TILE))),
        scratch_shapes=[
            pltpu.VMEM((len(parts) * SIDE * BLOCK, half), BF),
            pltpu.SemaphoreType.DMA((len(parts),)),
        ],
        compiler_params=room(56),
        cost_estimate=cost(4 * height * parts[0].size, height * half * 8),
        name="contract",
    )(order, total, rows, *late, *parts)


def mix_kernel(places, own, total_ref, lefts_ref, *refs):
    count = len(places)
    weights, pieces, refs = refs[:2], refs[2 : 2 + count], refs[2 + count :]
    low_ref, raw_ref, square_ref, held, lows, weight, sems, weight_sems = refs
    i = pl.program_id(0)
    last = pl.num_programs(0) - 1
    tiles = last // CORES
    main = tiles * TALL_TILE
    copies = [
        piece_copy(pieces[n], 0, take, high, held.at[pl.ds(at, high), :], sems.at[n])
        for n, (take, at, high) in enumerate(places)
    ]
    high = weights[0].shape[0]
    loads = [
        pltpu.make_async_copy(part, weight.at[pl.ds(n * high, high), :], weight_sems.at[n])
        for n, part in enumerate(weights)
    ]

    @pl.when(i == 0)
    def _():
        for copy in loads + copies:
            copy.start()
        for load in loads:
            load.wait()

    def finish(resid):
        rows = pl.ds(pl.multiple_of(i * TALL_TILE, TALL_TILE), TALL_TILE)
        value = total_ref[...].astype(F32) + dot(lefts_ref[...], weight[...], NN)
        if resid is not None:
            value = value + resid.astype(F32)
        low = value.astype(BF)
        low_ref[...] = low
        lows[rows, :] = low
        squares = jnp.sum(value * value, axis=1, keepdims=True)
        square_ref[...] = jnp.broadcast_to(squares, (TALL_TILE, BLOCK)).T[: MARK[0]]

    plain = (i % tiles != tiles - 1) & (i != last)

    @pl.when(plain)
    def _():
        finish(None)

    @pl.when(jnp.logical_not(plain))
    def _():
        which = jnp.where(i == last, CORES, i // tiles)
        for e in range(3):

            @pl.when(which == e)
            def _():
                for n, place in enumerate(places):
                    if place[1] // TALL_TILE == e:
                        copies[n].wait()

        finish(held[pl.ds(pl.multiple_of(which * TALL_TILE, TALL_TILE), TALL_TILE), :])

    for e in range(CORES):
        base = e * main

        @pl.when(i == (e + 1) * tiles - 1)
        def _():
            raw_ref[e, : main - own] = dot(
                lows[base + own : base + main, :], lows[base : base + own, :], NT
            )

        @pl.when(i == last)
        def _():
            start = CORES * main + e * BLOCK
            raw_ref[e, main - own :] = dot(
                lows[start : start + BLOCK, :], lows[base : base + own, :], NT
            )


def mix(total, lefts, parts, pieces, places, own):
    height, half = total.shape
    tile = lambda width: pl.BlockSpec((TALL_TILE, width), lambda i: (i, 0))
    raw = (CORES, height // CORES - own, own)
    return pl.pallas_call(
        lambda *refs: mix_kernel(places, own, *refs),
        out_shape=(
            jax.ShapeDtypeStruct((height, half), BF),
            jax.ShapeDtypeStruct(raw, F32),
            jax.ShapeDtypeStruct((MARK[0], height), F32),
        ),
        grid=(height // TALL_TILE,),
        in_specs=[tile(half), tile(lefts.shape[1])] + [ANYWHERE] * (len(parts) + len(pieces)),
        out_specs=(
            tile(half),
            whole(raw),
            pl.BlockSpec((MARK[0], TALL_TILE), lambda i: (0, i)),
        ),
        scratch_shapes=[
            pltpu.VMEM((3 * TALL_TILE, half), BF),
            pltpu.VMEM((height, half), BF),
            pltpu.VMEM((SIDE * BLOCK, half), BF),
            pltpu.SemaphoreType.DMA((len(pieces),)),
            pltpu.SemaphoreType.DMA((len(parts),)),
        ],
        compiler_params=room(56),
        cost_estimate=cost(2 * height * 512 * half, height * half * 10),
        name="mix",
    )(total, lefts, *parts, *pieces)


def project_kernel(low_ref, grad_q_ref, grad_p_ref, coef_ref, delta_ref):
    cores, queries, own = grad_q_ref.shape
    main = (low_ref.shape[0] - cores * BLOCK) // cores
    for e in range(cores):
        coef = coef_ref[e].T
        base, tail = e * main, cores * main + e * BLOCK
        low_p = low_ref[base : base + own]
        low_q = low_ref[base + own : base + main]
        low_t = low_ref[tail : tail + BLOCK]
        near = main - own
        up_p = dot(grad_p_ref[e], jnp.concatenate([low_q, low_t], axis=0), TN)
        up_q = dot(grad_q_ref[e], low_p, NN)
        delta_ref[base : base + own] = (
            up_p * coef[:own, 0:1] - low_p.astype(F32) * coef[:own, 1:2]
        ).astype(BF)
        delta_ref[base + own : base + main] = (
            up_q[:near] * coef[own:main, 0:1] - low_q.astype(F32) * coef[own:main, 1:2]
        ).astype(BF)
        delta_ref[tail : tail + BLOCK] = (
            up_q[near:] * coef[main:, 0:1] - low_t.astype(F32) * coef[main:, 1:2]
        ).astype(BF)


def project(low, grad_q, grad_p, coef):
    height, half = low.shape
    slab = half // 4
    block = pl.BlockSpec((height, slab), lambda h: (0, h))
    return pl.pallas_call(
        project_kernel,
        out_shape=jax.ShapeDtypeStruct(low.shape, BF),
        grid=(4,),
        in_specs=[block, whole(grad_q.shape), whole(grad_p.shape), whole(coef.shape)],
        out_specs=block,
        compiler_params=room(24),
        cost_estimate=cost(4 * grad_q.size * half, low.size * 4),
        name="project",
    )(low, grad_q, grad_p, coef)


def term_kernel(groups, added, order_ref, *refs):
    count = sum(len(picks) for picks in groups)
    lefts, rests, refs = refs[:count], refs[count : 2 * count], refs[2 * count :]
    delta_ref, adds = refs[0], refs[1 : 1 + added]
    outs, (mark_ref, left) = refs[-2 - len(groups) : -2], refs[-2:]
    mark_ref[...] = jnp.zeros_like(mark_ref)
    main = lefts[0].shape[1]

    @pl.when(pl.program_id(0) == 0)
    def _():
        for k in range(count):
            left[k * BLOCK : (k + 1) * BLOCK, :main] = lefts[k][...]
            left[k * BLOCK : (k + 1) * BLOCK, main:] = rests[k][...]

    value = dot(left[...], delta_ref[...], NN)
    at = 0
    for n, out_ref in enumerate(outs):
        height = out_ref.shape[0]
        part = value[at : at + height]
        if added:
            part = part + adds[n][...].astype(F32)
        out_ref[...] = part.astype(BF)
        at += height


def term(order, turned, delta, groups, adds=(), after=()):
    height, half = delta.shape
    slab = half // 4
    picks = [n for group in groups for n in group]
    lefts = [
        pl.BlockSpec(
            (BLOCK, v.shape[1]), lambda i, o, n=n: (o[n], 0), pipeline_mode=pl.Buffered(1)
        )
        for v in turned
        for n in picks
    ]
    sizes = [len(group) * BLOCK for group in groups]
    count = len(picks)
    return pl.pallas_call(
        lambda *refs: term_kernel(groups, len(adds), *refs),
        out_shape=[jax.ShapeDtypeStruct((size, half), BF) for size in sizes] + [MARKED],
        grid_spec=pltpu.PrefetchScalarGridSpec(
            num_scalar_prefetch=1,
            grid=(4,),
            in_specs=lefts
            + [pl.BlockSpec((height, slab), lambda i, o: (0, i))]
            + [pl.BlockSpec((v.shape[0], slab), lambda i, o: (0, i)) for v in adds]
            + [whole(MARK)] * len(after),
            out_specs=[pl.BlockSpec((size, slab), lambda i, o: (0, i)) for size in sizes]
            + [whole(MARK)],
            scratch_shapes=[pltpu.VMEM((count * BLOCK, height), BF)],
        ),
        compiler_params=room(24),
        cost_estimate=cost(2 * height * count * BLOCK * half, height * (half + 512) * 2),
        name="term",
    )(order, *([turned[0]] * count), *([turned[1]] * count), delta, *adds, *after)


def settle_kernel(own_ref, *refs):
    refs[-1][...] = jnp.zeros_like(refs[-1])
    for n in range(2):
        one, two = refs[2 * n], refs[2 * n + 1]
        height = one.shape[0]
        value = own_ref[n * height : (n + 1) * height].astype(F32)
        value = value + one[...].astype(F32) + two[...].astype(F32)
        for k in range(2):
            refs[-SIDE - 1 + 2 * n + k][...] = value[k * BLOCK : (k + 1) * BLOCK].astype(BF)


def settle(own, tops, bottoms, after):
    height, half = own.shape
    slab = half // 4
    part = pl.BlockSpec((height // 2, slab), lambda i: (0, i))
    return pl.pallas_call(
        settle_kernel,
        out_shape=[jax.ShapeDtypeStruct((BLOCK, half), BF)] * SIDE + [MARKED],
        grid=(4,),
        in_specs=[pl.BlockSpec((height, slab), lambda i: (0, i))]
        + [part] * 4
        + [whole(MARK)] * len(after),
        out_specs=[pl.BlockSpec((BLOCK, slab), lambda i: (0, i))] * SIDE + [whole(MARK)],
        compiler_params=room(16),
        cost_estimate=cost(0, 8 * MIB),
        name="settle",
    )(own, *tops, *bottoms, *after)


def gather_kernel(*refs):
    value = refs[0][...].astype(F32)
    for ref in refs[1:SIDE]:
        value = value + ref[...].astype(F32)
    refs[-1][...] = value.astype(BF)


def gather(blocks, after):
    height, half = blocks[0].shape
    tile = pl.BlockSpec((height, half // 2), lambda i: (0, i))
    return pl.pallas_call(
        gather_kernel,
        out_shape=jax.ShapeDtypeStruct((height, half), BF),
        grid=(2,),
        in_specs=[tile] * SIDE + [whole(MARK)],
        out_specs=tile,
        compiler_params=room(12),
        cost_estimate=cost(0, 4 * MIB),
        name="gather",
    )(*blocks, after)


def back_kernel(order_ref, own_rows_ref, other_rows_ref, *refs):
    weights, (own_ref, other_ref, mark_ref, held, sems) = refs[: SIDE + 1], refs[-5:]
    mark_ref[...] = jnp.zeros_like(mark_ref)
    copies, at = [], 0
    for n, weight in enumerate(weights):
        height = weight.shape[0]
        copies.append(
            pltpu.make_async_copy(weight, held.at[pl.ds(at, height), :], sems.at[n])
        )
        copies[-1].start()
        at += height
    at = 0
    rows = own_ref.shape[0]
    left = jnp.concatenate([own_rows_ref[...], other_rows_ref[...]], axis=0)
    for n, weight in enumerate(weights):
        height = weight.shape[0]
        copies[n].wait()
        value = dot(left, held[at : at + height, :], NT)
        for k in range(height // BLOCK):
            place = columns(order_ref, at // BLOCK + k)
            piece = value[:, k * BLOCK : (k + 1) * BLOCK]
            own_ref[:, place] = piece[:rows]
            other_ref[:, place] = piece[rows:].astype(BF)
        at += height


def back(order, own, other, height, parts, after):
    half = own[0].shape[1]
    depth = sum(part.shape[0] for part in parts)
    return pl.pallas_call(
        back_kernel,
        out_shape=(
            jax.ShapeDtypeStruct((height, depth), F32),
            jax.ShapeDtypeStruct((height, depth), BF),
            MARKED,
        ),
        grid=(1,),
        in_specs=[SCALARS]
        + [pl.BlockSpec((height, half), lambda i, n=n: (n, 0)) for _, n in (own, other)]
        + [ANYWHERE] * len(parts)
        + [whole(MARK)] * len(after),
        out_specs=(whole((height, depth)), whole((height, depth)), whole(MARK)),
        scratch_shapes=[
            pltpu.VMEM((depth, half), BF),
            pltpu.SemaphoreType.DMA((len(parts),)),
        ],
        compiler_params=room(28),
        cost_estimate=cost(4 * height * depth * half, 14 * MIB),
        name="back",
    )(order, own[0], other[0], *parts, *after)


def combine_kernel(own_ref, got_ref, out_ref, mark_ref):
    mark_ref[...] = jnp.zeros_like(mark_ref)
    out_ref[...] = (own_ref[...] + got_ref[...].astype(F32)).astype(BF)


def combine(own, got):
    height, depth = own.shape
    tile = pl.BlockSpec((height, depth // 4), lambda i: (0, i))
    return pl.pallas_call(
        combine_kernel,
        out_shape=(jax.ShapeDtypeStruct(own.shape, BF), MARKED),
        grid=(4,),
        in_specs=[tile, tile],
        out_specs=(tile, whole(MARK)),
        compiler_params=room(12),
        cost_estimate=cost(0, 8 * height * depth),
        name="combine",
    )(own, got)


def lay_kernel(core_ref, own_ref, got_ref, out_ref, mark_ref):
    i = pl.program_id(0)
    mark_ref[...] = jnp.zeros_like(mark_ref)

    @pl.when(i < 2)
    def _():
        out_ref[...] = own_ref[...]

    @pl.when(i >= 2)
    def _():
        out_ref[...] = got_ref[...]


def lay(core, delta, got):
    height, half = got.shape
    quarter = half // 2
    return pl.pallas_call(
        lay_kernel,
        out_shape=(jax.ShapeDtypeStruct((height, 4 * quarter), BF), MARKED),
        grid_spec=pltpu.PrefetchScalarGridSpec(
            num_scalar_prefetch=1,
            grid=(4,),
            in_specs=[
                pl.BlockSpec((height, quarter), lambda i, core: (0, jnp.minimum(i, 1))),
                pl.BlockSpec((height, quarter), lambda i, core: (0, jnp.maximum(i - 2, 0))),
            ],
            out_specs=(pl.BlockSpec(
                (height, quarter),
                lambda i, core: (0, jnp.where(i < 2, 2 * core[0], 2 * (1 - core[0]) - 2) + i),
            ), whole(MARK)),
        ),
        compiler_params=room(12),
        cost_estimate=cost(0, 16 * height * quarter),
        name="lay",
    )(core, delta, got)


def body(query_attn, query_resid, passage_attn, passage_resid, out_weight, hard_lists, positive):
    z = lax.axis_index("dp")
    f = lax.axis_index("fsdp")
    c, x, y = f % CORES, (f // CORES) % SIDE, f // (SIDE * CORES)
    first = c == 0
    width = query_resid.shape[1]
    half = width // 2
    own_rows = passage_attn.shape[0]
    blocks = own_rows // BLOCK

    core = c.astype(jnp.int32).reshape(1)

    got = swap(other_halves(core, [out_weight, query_resid]))
    shard = chip_shard(core, out_weight, got)
    near = [shard, first_up(shard), first_down(shard), first_across(shard)]
    hops = jnp.array(HOPS, jnp.int32)
    ys, xs = (y + hops) % SIDE, (x + hops) % SIDE
    order = jnp.where(
        first, ys[:, None] * SIDE + xs[None, :], ys[None, :] * SIDE + xs[:, None]
    )
    order = order.reshape(-1).astype(jnp.int32)

    leading = lead(core, query_attn, query_resid)
    near_up, near_down = z_up(leading), z_down(leading)
    resid = pair_rows(core, query_resid, got)
    numbers = jnp.concatenate([hard_lists.reshape(-1), positive])
    other_numbers = swap(numbers)
    to_up, to_down, three = pack(query_attn, near_up, near_down, resid)
    from_up, from_down = z_up(to_up), z_down(to_down)
    weight = stack(near)
    parts = [weight, second_up(weight), second_down(weight)]
    pieces = [passage_attn, three, swap(passage_attn), swap(three)]
    main = own_rows + 3 * BLOCK
    places = [
        (0, 0, own_rows),
        (0, own_rows, 3 * BLOCK),
        (0, main, own_rows),
        (0, main + own_rows, 3 * BLOCK),
    ]
    span = own_rows + BLOCK
    other_resid = swap(other_half(core, passage_resid))
    resid_pieces = [passage_resid, resid, other_resid, resid]
    resid_places = [
        (None, 0, own_rows),
        (0, own_rows, BLOCK),
        (0, span, own_rows),
        (BLOCK, span + own_rows, BLOCK),
    ]
    total, rows, turned, mark = begin(
        order, core, weight, pieces, places, resid_pieces, resid_places
    )
    on_up, on_down = halves(parts[1], parts[2], [mark])
    parts += [second_up(on_up), second_down(on_down)]
    resid_up, resid_down, attn_far = repack(near_up, from_up, from_down, other_numbers)
    far_up, far_down = z_up(resid_up), z_down(resid_down)
    late = [attn_far, swap(attn_far)]

    total, lefts, turned_far = contract(order, total, rows, late, parts[:3])
    turned = (turned, turned_far)
    part = BLOCK // 2
    pieces = [near_up, near_down, from_up, from_down, far_up, far_down]
    places = [(BLOCK if n < 2 else part, n * BLOCK, BLOCK) for n in range(4)]
    places += [(0, n * BLOCK, BLOCK) for n in (4, 5)]
    low, raw, squares = mix(total, lefts, parts[3:], pieces, places, own_rows)
    squares = squares[0]
    raw = raw.reshape(CORES, SIDE, BLOCK, own_rows)

    squares = squares + jnp.concatenate(
        [squares_in for squares_in in (lambda v: (
            v[main : 2 * main], v[:main], v[2 * main + BLOCK :], v[2 * main : 2 * main + BLOCK]
        ))(swap(squares))]
    )
    squares = jnp.concatenate(
        [squares[: CORES * main].reshape(CORES, main), squares[CORES * main :].reshape(CORES, BLOCK)],
        axis=1,
    )
    squares_p = squares[:, :own_rows]
    squares_q = squares[:, own_rows:].reshape(CORES, SIDE, BLOCK)
    raw = raw + swap(raw)[::-1]
    factor_p = lax.rsqrt(squares_p + epsilon)
    factor_q = lax.rsqrt(squares_q + epsilon)

    listed = hard_lists.size
    lists = jnp.stack([numbers[:listed], other_numbers[:listed]]).reshape(CORES, SIDE, -1)
    ks = jnp.arange(SIDE, dtype=jnp.int32)
    source = (z + hops) % SIDE
    asked = jnp.take(lists, source, axis=1)
    ids = z * blocks + jnp.arange(blocks, dtype=jnp.int32)
    wanted = jnp.any(asked[:, :, :, None] == ids, axis=2)
    wanted = wanted | (ks == 0)[None, :, None]
    wanted = jnp.repeat(wanted, BLOCK, axis=2)[:, :, None, :]
    hits = jnp.stack([numbers[listed:], other_numbers[listed:]])
    target = (jnp.arange(own_rows, dtype=jnp.int32) == hits[:, :, None])[:, None]
    target = (target & (ks == 0)[None, :, None, None]).astype(F32)

    scores = sharpness * raw * factor_q[..., None] * factor_p[:, None, None, :]
    scores = jnp.where(wanted, scores, -1e30)
    highest = jnp.max(scores, axis=3)
    totals = jnp.sum(jnp.exp(scores - highest[..., None]), axis=3)
    stats = jnp.stack([highest, totals])
    all_stats = [stats]
    for k in range(1, SIDE):
        got = z_to[-HOPS[k] % SIDE](stats)
        picks = [[h % SIDE for h in HOPS].index((h - HOPS[k]) % SIDE) for h in HOPS]
        all_stats.append(jnp.concatenate([got[:, :, i : i + 1] for i in picks], axis=2))
    top = all_stats[0][0]
    for v in all_stats[1:]:
        top = jnp.maximum(top, v[0])
    log_total = top + jnp.log(sum(v[1] * jnp.exp(v[0] - top) for v in all_stats))
    query_loss = log_total[0, 0] - jnp.sum(scores[0, 0] * target[0, 0], axis=1)

    scale = sharpness / (BLOCK * DEVICES)
    grad = scale * (jnp.exp(scores - log_total[..., None]) - target)
    weighted = grad * scores * (1.0 / sharpness)
    inner_q = jnp.sum(weighted, axis=3)
    inner_p = jnp.sum(weighted, axis=(1, 2))
    grad_q = (grad * factor_p[:, None, None, :]).astype(BF).reshape(CORES, -1, own_rows)
    grad_p = (grad * factor_q[..., None]).astype(BF).reshape(CORES, -1, own_rows)
    factors = jnp.concatenate([factor_p, factor_q.reshape(CORES, -1)], axis=1)
    inners = jnp.concatenate([inner_p, inner_q.reshape(CORES, -1)], axis=1)
    coef = jnp.stack([factors, factors * factors * inners], axis=1)
    delta = project(low, grad_q, grad_p, coef)

    def at(e, j):
        return (e * main + own_rows) // BLOCK + j

    def both(e, j, k):
        return at(e, j), at(e, k)

    end = CORES * main // BLOCK
    far_top, far_bottom, mark = term(order, turned, delta, ((12, 13), (14, 15)))
    up, down = second_up(far_top), second_down(far_bottom)
    far, _ = join(core, delta, [((end + e,) * 2,) for e in range(CORES)], after=[mark])
    far = z_with(far)
    up_bottom, down_top, mark = term(
        order, turned, delta, ((10, 11), (4, 5)), after=[mark]
    )
    got_bottom, got_top = second_up(up_bottom), second_down(down_top)
    blocks = own_rows // BLOCK
    kept = [(both(0, k, k),) for k in range(-blocks, 1)] + [(both(1, 0, 0),)]
    mine, kept_mark = join(core, delta, kept, after=[mark])
    theirs, mark = join(
        core, delta, [(both(1, k, k),) for k in range(-blocks, 0)], after=[kept_mark]
    )
    up_top, down_bottom, mark = term(
        order, turned, delta, ((8, 9), (6, 7)), [up, down], [mark]
    )
    passage_delta, lay_mark = lay(core, mine, swap(theirs))
    got_tops = [got_top, second_up(up_top)]
    got_bottoms = [got_bottom, second_down(down_bottom)]
    own_sum, mark = term(order, turned, delta, ((0, 1, 2, 3),), after=[mark])
    flow, mark = join(
        core, delta, [(both(e, 2, 1), (0, e)) for e in range(CORES)], [far], [mark]
    )
    counter, counter_mark = join(
        core, delta, [(both(e, 1, 2),) for e in range(CORES)], after=[mark]
    )
    z_got = [z_with(flow), z_against(counter)]
    *sums, mark = settle(own_sum, got_tops, got_bottoms, [mark, counter_mark, lay_mark])
    own_back, other_back, back_mark = back(
        order, (mine, 0), (theirs, 0), own_rows, parts, [mark]
    )
    summed, _ = join(
        core,
        mine,
        [((blocks + e,) * 2, (0, e), (1, e)) for e in range(CORES)],
        z_got,
        [back_mark],
    )
    got = [sums[0], first_down(sums[1]), first_up(sums[2]), first_across(sums[3])]
    part = gather(got, back_mark)
    part = part.reshape(CORES, SIDE, BLOCK // 8, half)

    def pick(v, index, axis):
        return lax.dynamic_index_in_dim(v, index, axis, keepdims=False)

    total = pick(part, z, 1).astype(F32)
    for k in (1, 3, 2):
        total = total + z_to[k](pick(part, (z + k) % SIDE, 1)).astype(F32)
    total = total.astype(BF)
    own, other = pick(total, c, 0), swap(pick(total, 1 - c, 0))
    total = jnp.where(
        first, jnp.concatenate([own, other], axis=1), jnp.concatenate([other, own], axis=1)
    )
    late_mark = total[: MARK[0], : MARK[1]].astype(F32)
    weight_grad = jnp.zeros((SIDE,) + total.shape, F32)
    for k in (0, 1, 3, 2):
        got = total if k == 0 else z_to[k](total)
        weight_grad = lax.dynamic_update_index_in_dim(
            weight_grad, got.astype(F32), (z - k) % SIDE, 0
        )
    weight_grad = weight_grad.reshape(out_weight.shape)

    passage_back, back_mark = combine(own_back, swap(other_back))
    own_back, other_back, _ = back(
        order, (summed, 0), (summed, 1), BLOCK, parts, [late_mark]
    )
    query_back, _ = combine(own_back, swap(other_back))
    query_delta, _ = lay(core, summed, swap(summed[BLOCK:]))
    return (query_loss, query_back, query_delta, passage_back, passage_delta, weight_grad)


def solution(mesh):
    rows = P(("dp", "fsdp"), None)
    return jax.shard_map(
        body,
        mesh=mesh,
        in_specs=(
            rows,
            rows,
            rows,
            rows,
            P("fsdp", None),
            P("fsdp", None, None),
            P(("dp", "fsdp")),
        ),
        out_specs=(P(("dp", "fsdp")), rows, rows, rows, rows, P("fsdp", None)),
        check_vma=False,
    )
```

```python
import jax
import jax.numpy as jnp
from jax import lax
from jax.experimental import pallas as pl
from jax.experimental.pallas import tpu as pltpu
from jax.sharding import PartitionSpec as P

BLOCK = 128
SIDE = 4
CORES = 2
FSDP = SIDE * SIDE * CORES
DEVICES = SIDE * FSDP

sharpness = 250.0
epsilon = 1e-06
BF = jnp.bfloat16
F32 = jnp.float32


def route(target):
    pairs = []
    for source in range(DEVICES):
        z, rest = divmod(source, FSDP)
        y, rest = divmod(rest, SIDE * CORES)
        x, c = divmod(rest, CORES)
        z, y, x, c = target(z, y, x, c)
        pairs.append((source, (((z % SIDE) * SIDE + y % SIDE) * SIDE + x % SIDE) * CORES + c))
    return lambda value: lax.ppermute(value, ("dp", "fsdp"), pairs)


def way(c):
    return 1 - 2 * c


def along_first(shift):
    return route(
        lambda z, y, x, c: (z, y, x + shift, c) if c == 0 else (z, y + shift, x, c)
    )


def along_second(shift):
    return route(
        lambda z, y, x, c: (z, y + shift, x, c) if c == 0 else (z, y, x + shift, c)
    )


swap = route(lambda z, y, x, c: (z, y, x, 1 - c))
z_to = [route(lambda z, y, x, c, k=k: (z + k, y, x, c)) for k in range(SIDE)]
z_up, z_across, z_down = z_to[1:]
z_with = route(lambda z, y, x, c: (z + way(c), y, x, c))
z_against = route(lambda z, y, x, c: (z - way(c), y, x, c))
first_up, first_down, first_across = (along_first(shift) for shift in (1, -1, 2))
second_up, second_down = (along_second(shift) for shift in (1, -1))


def dot(a, b, dims, batch=((), ())):
    return lax.dot_general(a, b, (dims, batch), preferred_element_type=F32)


TALL_TILE = 256
MIB = 1024 * 1024
HOPS = (0, -1, 1, 2)
ANYWHERE = pl.BlockSpec(memory_space=pl.ANY)
SCALARS = pl.BlockSpec(memory_space=pltpu.SMEM)
NT = ((1,), (1,))
NN = ((1,), (0,))
TN = ((0,), (0,))


def cost(flops, traffic):
    return pl.CostEstimate(
        flops=int(flops) // 4, bytes_accessed=int(traffic) // 4, transcendentals=0
    )


def room(mib):
    return pltpu.CompilerParams(vmem_limit_bytes=mib * MIB)


def whole(shape):
    return pl.BlockSpec(shape, lambda *_: (0,) * len(shape), pipeline_mode=pl.Buffered(1))


MARK = (8, BLOCK)
MARKED = jax.ShapeDtypeStruct(MARK, F32)


def copy_kernel(core_ref, in_ref, *refs):
    refs[-1][...] = in_ref[...]


def other_half(core, rows, after=()):
    height, half = rows.shape[0], rows.shape[1] // 2
    return pl.pallas_call(
        copy_kernel,
        out_shape=jax.ShapeDtypeStruct((height, half), rows.dtype),
        grid_spec=pltpu.PrefetchScalarGridSpec(
            num_scalar_prefetch=1,
            grid=(1,),
            in_specs=[pl.BlockSpec((height, half), lambda i, core: (0, 1 - core[0]))]
            + [ANYWHERE] * len(after),
            out_specs=pl.BlockSpec((height, half), lambda i, core: (0, 0)),
        ),
        compiler_params=room(12),
        cost_estimate=cost(0, 4 * height * half),
        name="other_half",
    )(core, rows, *after)


def halves_of_kernel(core_ref, *refs):
    at = 0
    for ref in refs[:-1]:
        refs[-1][at : at + ref.shape[0]] = ref[...]
        at += ref.shape[0]


def other_halves(core, arrays):
    half = arrays[0].shape[1] // 2
    shape = (sum(v.shape[0] for v in arrays), half)
    return pl.pallas_call(
        halves_of_kernel,
        out_shape=jax.ShapeDtypeStruct(shape, BF),
        grid_spec=pltpu.PrefetchScalarGridSpec(
            num_scalar_prefetch=1,
            grid=(1,),
            in_specs=[
                pl.BlockSpec((v.shape[0], half), lambda i, core: (0, 1 - core[0])) for v in arrays
            ],
            out_specs=whole(shape),
        ),
        compiler_params=room(8),
        cost_estimate=cost(0, 4 * shape[0] * half),
        name="other_halves",
    )(core, *arrays)


def shard_kernel(core_ref, own_ref, got_ref, out_ref):
    core = core_ref[0]
    height = own_ref.shape[0]
    for rows, at in ((own_ref, core), (got_ref, 1 - core)):
        out_ref[pl.ds(pl.multiple_of(at * height, height), height), :] = rows[:height]


def chip_shard(core, weight, got):
    height, half = weight.shape[0], got.shape[1]
    return pl.pallas_call(
        shard_kernel,
        out_shape=jax.ShapeDtypeStruct((CORES * height, half), weight.dtype),
        grid_spec=pltpu.PrefetchScalarGridSpec(
            num_scalar_prefetch=1,
            grid=(1,),
            in_specs=[
                pl.BlockSpec((height, half), lambda i, core: (0, core[0])),
                whole(got.shape),
            ],
            out_specs=whole((CORES * height, half)),
        ),
        compiler_params=room(12),
        cost_estimate=cost(0, 8 * height * half),
        name="chip_shard",
    )(core, weight, got)


def pair_rows_kernel(core_ref, own_ref, got_ref, out_ref):
    height = own_ref.shape[0]
    out_ref[:height] = own_ref[...]
    out_ref[height:] = got_ref[got_ref.shape[0] - height :]


def pair_rows(core, rows, got):
    height, half = rows.shape[0], got.shape[1]
    return pl.pallas_call(
        pair_rows_kernel,
        out_shape=jax.ShapeDtypeStruct((CORES * height, half), rows.dtype),
        grid_spec=pltpu.PrefetchScalarGridSpec(
            num_scalar_prefetch=1,
            grid=(1,),
            in_specs=[pl.BlockSpec((height, half), lambda i, core: (0, core[0])), whole(got.shape)],
            out_specs=whole((CORES * height, half)),
        ),
        compiler_params=room(12),
        cost_estimate=cost(0, 8 * height * half),
        name="pair_rows",
    )(core, rows, got)


def columns(order_ref, i):
    return pl.ds(pl.multiple_of(order_ref[i] * BLOCK, BLOCK), BLOCK)


def lead_kernel(core_ref, attn_ref, resid_ref, out_ref):
    out_ref[:BLOCK] = attn_ref[...]
    out_ref[BLOCK:] = resid_ref[...]


def lead(core, attn, resid):
    shape = (2 * BLOCK, attn.shape[1])
    return pl.pallas_call(
        lead_kernel,
        out_shape=jax.ShapeDtypeStruct(shape, BF),
        grid_spec=pltpu.PrefetchScalarGridSpec(
            num_scalar_prefetch=1,
            grid=(1,),
            in_specs=[
                whole(attn.shape),
                pl.BlockSpec(attn.shape, lambda i, core: (0, core[0])),
            ],
            out_specs=whole(shape),
        ),
        compiler_params=room(8),
        cost_estimate=cost(0, 2 * MIB),
        name="lead",
    )(core, attn, resid)


def pack_kernel(attn_ref, up_ref, down_ref, resid_ref, to_up, to_down, three_ref):
    part = BLOCK // 2
    to_up[:part] = up_ref[:part]
    to_up[part:] = resid_ref[...]
    to_down[:part] = down_ref[part:BLOCK]
    to_down[part:] = resid_ref[...]
    for n, row in enumerate((attn_ref, up_ref, down_ref)):
        three_ref[n * BLOCK : (n + 1) * BLOCK] = row[:BLOCK]


def pack(attn, up, down, resid):
    half = attn.shape[1]
    shapes = [(BLOCK // 2 + BLOCK, half)] * 2 + [(3 * BLOCK, half)]
    operands = [attn, up, down]
    last = resid.shape[0] // BLOCK - 1
    return pl.pallas_call(
        pack_kernel,
        out_shape=[jax.ShapeDtypeStruct(s, BF) for s in shapes],
        grid=(1,),
        in_specs=[whole(v.shape) for v in operands]
        + [pl.BlockSpec((BLOCK, half), lambda i: (last, 0))],
        out_specs=[whole(s) for s in shapes],
        compiler_params=room(56),
        cost_estimate=cost(0, 8 * MIB),
        name="pack",
    )(*operands, resid)


def stack_kernel(*refs):
    out_ref = refs[-1]
    for n, row in enumerate(refs[:-1]):
        out_ref[n * BLOCK : (n + 1) * BLOCK] = row[...]


def stack(blocks):
    half = blocks[0].shape[1]
    shape = (len(blocks) * BLOCK, half)
    return pl.pallas_call(
        stack_kernel,
        out_shape=jax.ShapeDtypeStruct(shape, BF),
        grid=(1,),
        in_specs=[whole(v.shape) for v in blocks],
        out_specs=whole(shape),
        compiler_params=room(16),
        cost_estimate=cost(0, 4 * MIB),
        name="stack",
    )(*blocks)


def halves_kernel(one_ref, two_ref, *refs):
    refs[-2][...] = one_ref[...]
    refs[-1][...] = two_ref[...]


def halves(one, two, after):
    height, half = one.shape
    shape = (height // 2, half)
    return pl.pallas_call(
        halves_kernel,
        out_shape=[jax.ShapeDtypeStruct(shape, BF)] * 2,
        grid=(1,),
        in_specs=[
            pl.BlockSpec(shape, lambda i: (0, 0)),
            pl.BlockSpec(shape, lambda i: (1, 0)),
        ]
        + [whole(MARK)] * len(after),
        out_specs=[whole(shape)] * 2,
        compiler_params=room(16),
        cost_estimate=cost(0, 8 * MIB),
        name="halves",
    )(one, two, *after)


def repack_kernel(near_ref, up_ref, down_ref, *refs):
    outs = refs[-3:]
    part = BLOCK // 2
    outs[0][...] = near_ref[...]
    outs[1][...] = down_ref[part:]
    outs[2][:part] = up_ref[:part]
    outs[2][part:] = down_ref[:part]


def repack(near, up, down, after):
    shape = (BLOCK, up.shape[1])
    return pl.pallas_call(
        repack_kernel,
        out_shape=[jax.ShapeDtypeStruct(shape, BF)] * 3,
        grid=(1,),
        in_specs=[
            pl.BlockSpec(shape, lambda i: (1, 0)),
            whole(up.shape),
            whole(down.shape),
            ANYWHERE,
        ],
        out_specs=[whole(shape)] * 3,
        compiler_params=room(12),
        cost_estimate=cost(0, 6 * MIB),
        name="repack",
    )(near, up, down, after)


def join_kernel(picks, core_ref, *refs):
    count = len(picks)
    out_ref, mark_ref = refs[-2:]
    mark_ref[...] = jnp.zeros_like(mark_ref)
    for n, (_, *more) in enumerate(picks):
        place = slice(n * BLOCK, (n + 1) * BLOCK)
        value = refs[n][...]
        for add, at in more:
            value = value.astype(F32) + refs[count + add][at * BLOCK : (at + 1) * BLOCK].astype(F32)
        out_ref[place] = value.astype(BF)


def join(core, delta, picks, adds=(), after=()):
    half = delta.shape[1]
    shape = (len(picks) * BLOCK, half)

    def block(numbers):
        return pl.BlockSpec(
            (BLOCK, half), lambda i, c: (jnp.where(c[0] == 0, numbers[0], numbers[1]), 0)
        )

    return pl.pallas_call(
        lambda *refs: join_kernel(picks, *refs),
        out_shape=(jax.ShapeDtypeStruct(shape, BF), MARKED),
        grid_spec=pltpu.PrefetchScalarGridSpec(
            num_scalar_prefetch=1,
            grid=(1,),
            in_specs=[block(pick[0]) for pick in picks]
            + [whole(v.shape) for v in adds]
            + [whole(MARK)] * len(after),
            out_specs=(whole(shape), whole(MARK)),
        ),
        compiler_params=room(20),
        cost_estimate=cost(0, 4 * MIB),
        name="join",
    )(core, *([delta] * len(picks)), *adds, *after)


def piece_copy(piece, core, take, height, target, sem):
    if take is None:
        half = target.shape[1]
        piece = piece.at[:, pl.ds(pl.multiple_of(core * half, half), half)]
    else:
        piece = piece.at[pl.ds(take, height), :]
    return pltpu.make_async_copy(piece, target, sem)


def picked(refs, order_ref, numbers):
    return jnp.concatenate(
        [
            jnp.concatenate([ref[:, columns(order_ref, n)] for n in numbers], axis=1)
            for ref in refs
        ],
        axis=0,
    )


def begin_kernel(places, resid_places, order_ref, core_ref, weight_ref, *refs):
    count = len(places) + len(resid_places)
    pieces, refs = refs[:count], refs[count:]
    total_ref, rows_ref, turned_ref, mark_ref, held, resid, sems = refs[-7:]
    i = pl.program_id(0)
    tiles = pl.num_programs(0) // CORES
    copies, groups = [], []
    for n, (take, at, high) in enumerate(places + resid_places):
        target = held if n < len(places) else resid
        copies.append(
            piece_copy(pieces[n], core_ref[0], take, high, target.at[pl.ds(at, high), :], sems.at[n])
        )
        groups.append(at * CORES // target.shape[0])

    @pl.when(i == 0)
    def _():
        for e in range(CORES):
            for n, copy in enumerate(copies):
                if groups[n] == e:
                    copy.start()

    for e in range(CORES):

        @pl.when(i == e * tiles)
        def _():
            for n, copy in enumerate(copies):
                if groups[n] == e:
                    copy.wait()

    tile = held.at[pl.ds(pl.multiple_of(i * TALL_TILE, TALL_TILE), TALL_TILE), :]
    rows = tile[...]
    rows_ref[...] = rows
    turned_ref[...] = rows.T
    mark_ref[...] = jnp.zeros_like(mark_ref)
    value = dot(picked([tile], order_ref, range(SIDE)), weight_ref[...], NN)
    with_resid = resid.shape[0] // CORES // TALL_TILE
    inside = i % tiles

    @pl.when(inside < with_resid)
    def _():
        at = pl.multiple_of((i // tiles * with_resid + inside) * TALL_TILE, TALL_TILE)
        total_ref[...] = (value + resid[pl.ds(at, TALL_TILE), :].astype(F32)).astype(BF)

    @pl.when(inside >= with_resid)
    def _():
        total_ref[...] = value.astype(BF)


def begin(order, core, weight, pieces, places, resid_pieces, resid_places):
    height = sum(place[2] for place in places)
    depth = pieces[0].shape[1]
    half = weight.shape[1]
    tile = lambda width: pl.BlockSpec((TALL_TILE, width), lambda i: (i, 0))
    count = len(pieces) + len(resid_pieces)
    return pl.pallas_call(
        lambda *refs: begin_kernel(places, resid_places, *refs),
        out_shape=(
            jax.ShapeDtypeStruct((height, half), BF),
            jax.ShapeDtypeStruct((height, depth), BF),
            jax.ShapeDtypeStruct((depth, height), BF),
            MARKED,
        ),
        grid=(height // TALL_TILE,),
        in_specs=[SCALARS, SCALARS, whole(weight.shape)] + [ANYWHERE] * count,
        out_specs=(
            tile(half),
            tile(depth),
            pl.BlockSpec((depth, TALL_TILE), lambda i: (0, i)),
            whole(MARK),
        ),
        scratch_shapes=[
            pltpu.VMEM((height, depth), BF),
            pltpu.VMEM((sum(place[2] for place in resid_places), half), BF),
            pltpu.SemaphoreType.DMA((count,)),
        ],
        compiler_params=room(48),
        cost_estimate=cost(2 * height * weight.size, 30 * MIB),
        name="begin",
    )(order, core, weight, *pieces, *resid_pieces)


def contract_kernel(order_ref, total_ref, rows_ref, own_ref, got_ref, *refs):
    weights, refs = refs[: SIDE - 1], refs[SIDE - 1 :]
    out_ref, last_ref, turned_ref, weight, sems = refs
    i = pl.program_id(0)
    last = pl.num_programs(0) - 1
    block = SIDE * BLOCK
    loads = [
        pltpu.make_async_copy(part, weight.at[pl.ds((n + 2) % 3 * block, block), :], sems.at[n])
        for n, part in enumerate(weights)
    ]

    @pl.when(i == 0)
    def _():
        for n in (1, 2, 0):
            loads[n].start()
        for n in (1, 2):
            loads[n].wait()

    later = range(SIDE, 3 * SIDE)
    final = range(3 * SIDE, 4 * SIDE)

    @pl.when(i < last)
    def _():
        value = dot(picked([rows_ref], order_ref, later), weight[: 2 * block, :], NN)
        out_ref[...] = (total_ref[...].astype(F32) + value).astype(BF)
        last_ref[...] = picked([rows_ref], order_ref, final)

    @pl.when(i == last)
    def _():
        loads[0].wait()
        late = [own_ref, got_ref]
        left = picked(late, order_ref, [*later, *range(SIDE)])
        out_ref[...] = dot(left, weight[...], NN).astype(BF)
        turned_ref[:, :BLOCK] = own_ref[...].T
        turned_ref[:, BLOCK:] = got_ref[...].T
        last_ref[...] = picked(late, order_ref, final)


def contract(order, total, rows, late, parts):
    height, depth = rows.shape
    half = total.shape[1]
    end = height // TALL_TILE - 1
    kept = lambda width: pl.BlockSpec((TALL_TILE, width), lambda i: (jnp.minimum(i, end), 0))
    tile = lambda width: pl.BlockSpec((TALL_TILE, width), lambda i: (i, 0))
    return pl.pallas_call(
        contract_kernel,
        out_shape=(
            jax.ShapeDtypeStruct((height + TALL_TILE, half), BF),
            jax.ShapeDtypeStruct((height + TALL_TILE, SIDE * BLOCK), BF),
            jax.ShapeDtypeStruct((depth, TALL_TILE), BF),
        ),
        grid=(end + 2,),
        in_specs=[SCALARS, kept(half), kept(depth)]
        + [whole(v.shape) for v in late]
        + [ANYWHERE] * len(parts),
        out_specs=(tile(half), tile(SIDE * BLOCK), whole((depth, TALL_TILE))),
        scratch_shapes=[
            pltpu.VMEM((len(parts) * SIDE * BLOCK, half), BF),
            pltpu.SemaphoreType.DMA((len(parts),)),
        ],
        compiler_params=room(56),
        cost_estimate=cost(4 * height * parts[0].size, height * half * 8),
        name="contract",
    )(order, total, rows, *late, *parts)


def mix_kernel(places, own, total_ref, lefts_ref, *refs):
    count = len(places)
    weights, pieces, refs = refs[:2], refs[2 : 2 + count], refs[2 + count :]
    low_ref, raw_ref, square_ref, held, lows, weight, sems, weight_sems = refs
    i = pl.program_id(0)
    last = pl.num_programs(0) - 1
    tiles = last // CORES
    main = tiles * TALL_TILE
    copies = [
        piece_copy(pieces[n], 0, take, high, held.at[pl.ds(at, high), :], sems.at[n])
        for n, (take, at, high) in enumerate(places)
    ]
    high = weights[0].shape[0]
    loads = [
        pltpu.make_async_copy(part, weight.at[pl.ds(n * high, high), :], weight_sems.at[n])
        for n, part in enumerate(weights)
    ]

    @pl.when(i == 0)
    def _():
        for copy in loads + copies:
            copy.start()
        for load in loads:
            load.wait()

    def finish(resid):
        rows = pl.ds(pl.multiple_of(i * TALL_TILE, TALL_TILE), TALL_TILE)
        value = total_ref[...].astype(F32) + dot(lefts_ref[...], weight[...], NN)
        if resid is not None:
            value = value + resid.astype(F32)
        low = value.astype(BF)
        low_ref[...] = low
        lows[rows, :] = low
        squares = jnp.sum(value * value, axis=1, keepdims=True)
        square_ref[...] = jnp.broadcast_to(squares, (TALL_TILE, BLOCK)).T[: MARK[0]]

    plain = (i % tiles != tiles - 1) & (i != last)

    @pl.when(plain)
    def _():
        finish(None)

    @pl.when(jnp.logical_not(plain))
    def _():
        which = jnp.where(i == last, CORES, i // tiles)
        for e in range(3):

            @pl.when(which == e)
            def _():
                for n, place in enumerate(places):
                    if place[1] // TALL_TILE == e:
                        copies[n].wait()

        finish(held[pl.ds(pl.multiple_of(which * TALL_TILE, TALL_TILE), TALL_TILE), :])

    for e in range(CORES):
        base = e * main

        @pl.when(i == (e + 1) * tiles - 1)
        def _():
            raw_ref[e, : main - own] = dot(
                lows[base + own : base + main, :], lows[base : base + own, :], NT
            )

        @pl.when(i == last)
        def _():
            start = CORES * main + e * BLOCK
            raw_ref[e, main - own :] = dot(
                lows[start : start + BLOCK, :], lows[base : base + own, :], NT
            )


def mix(total, lefts, parts, pieces, places, own):
    height, half = total.shape
    tile = lambda width: pl.BlockSpec((TALL_TILE, width), lambda i: (i, 0))
    raw = (CORES, height // CORES - own, own)
    return pl.pallas_call(
        lambda *refs: mix_kernel(places, own, *refs),
        out_shape=(
            jax.ShapeDtypeStruct((height, half), BF),
            jax.ShapeDtypeStruct(raw, F32),
            jax.ShapeDtypeStruct((MARK[0], height), F32),
        ),
        grid=(height // TALL_TILE,),
        in_specs=[tile(half), tile(lefts.shape[1])] + [ANYWHERE] * (len(parts) + len(pieces)),
        out_specs=(
            tile(half),
            whole(raw),
            pl.BlockSpec((MARK[0], TALL_TILE), lambda i: (0, i)),
        ),
        scratch_shapes=[
            pltpu.VMEM((3 * TALL_TILE, half), BF),
            pltpu.VMEM((height, half), BF),
            pltpu.VMEM((SIDE * BLOCK, half), BF),
            pltpu.SemaphoreType.DMA((len(pieces),)),
            pltpu.SemaphoreType.DMA((len(parts),)),
        ],
        compiler_params=room(56),
        cost_estimate=cost(2 * height * 512 * half, height * half * 10),
        name="mix",
    )(total, lefts, *parts, *pieces)


def project_kernel(low_ref, grad_q_ref, grad_p_ref, coef_ref, delta_ref):
    cores, queries, own = grad_q_ref.shape
    main = (low_ref.shape[0] - cores * BLOCK) // cores
    for e in range(cores):
        coef = coef_ref[e].T
        base, tail = e * main, cores * main + e * BLOCK
        low_p = low_ref[base : base + own]
        low_q = low_ref[base + own : base + main]
        low_t = low_ref[tail : tail + BLOCK]
        near = main - own
        up_p = dot(grad_p_ref[e], jnp.concatenate([low_q, low_t], axis=0), TN)
        up_q = dot(grad_q_ref[e], low_p, NN)
        delta_ref[base : base + own] = (
            up_p * coef[:own, 0:1] - low_p.astype(F32) * coef[:own, 1:2]
        ).astype(BF)
        delta_ref[base + own : base + main] = (
            up_q[:near] * coef[own:main, 0:1] - low_q.astype(F32) * coef[own:main, 1:2]
        ).astype(BF)
        delta_ref[tail : tail + BLOCK] = (
            up_q[near:] * coef[main:, 0:1] - low_t.astype(F32) * coef[main:, 1:2]
        ).astype(BF)


def project(low, grad_q, grad_p, coef):
    height, half = low.shape
    slab = half // 4
    block = pl.BlockSpec((height, slab), lambda h: (0, h))
    return pl.pallas_call(
        project_kernel,
        out_shape=jax.ShapeDtypeStruct(low.shape, BF),
        grid=(4,),
        in_specs=[block, whole(grad_q.shape), whole(grad_p.shape), whole(coef.shape)],
        out_specs=block,
        compiler_params=room(24),
        cost_estimate=cost(4 * grad_q.size * half, low.size * 4),
        name="project",
    )(low, grad_q, grad_p, coef)


def term_kernel(groups, added, order_ref, *refs):
    count = sum(len(picks) for picks in groups)
    lefts, rests, refs = refs[:count], refs[count : 2 * count], refs[2 * count :]
    delta_ref, adds = refs[0], refs[1 : 1 + added]
    outs, (mark_ref, left) = refs[-2 - len(groups) : -2], refs[-2:]
    mark_ref[...] = jnp.zeros_like(mark_ref)
    main = lefts[0].shape[1]

    @pl.when(pl.program_id(0) == 0)
    def _():
        for k in range(count):
            left[k * BLOCK : (k + 1) * BLOCK, :main] = lefts[k][...]
            left[k * BLOCK : (k + 1) * BLOCK, main:] = rests[k][...]

    value = dot(left[...], delta_ref[...], NN)
    at = 0
    for n, out_ref in enumerate(outs):
        height = out_ref.shape[0]
        part = value[at : at + height]
        if added:
            part = part + adds[n][...].astype(F32)
        out_ref[...] = part.astype(BF)
        at += height


def term(order, turned, delta, groups, adds=(), after=()):
    height, half = delta.shape
    slab = half // 2
    picks = [n for group in groups for n in group]
    lefts = [
        pl.BlockSpec(
            (BLOCK, v.shape[1]), lambda i, o, n=n: (o[n], 0), pipeline_mode=pl.Buffered(1)
        )
        for v in turned
        for n in picks
    ]
    sizes = [len(group) * BLOCK for group in groups]
    count = len(picks)
    return pl.pallas_call(
        lambda *refs: term_kernel(groups, len(adds), *refs),
        out_shape=[jax.ShapeDtypeStruct((size, half), BF) for size in sizes] + [MARKED],
        grid_spec=pltpu.PrefetchScalarGridSpec(
            num_scalar_prefetch=1,
            grid=(2,),
            in_specs=lefts
            + [pl.BlockSpec((height, slab), lambda i, o: (0, i))]
            + [pl.BlockSpec((v.shape[0], slab), lambda i, o: (0, i)) for v in adds]
            + [whole(MARK)] * len(after),
            out_specs=[pl.BlockSpec((size, slab), lambda i, o: (0, i)) for size in sizes]
            + [whole(MARK)],
            scratch_shapes=[pltpu.VMEM((count * BLOCK, height), BF)],
        ),
        compiler_params=room(24),
        cost_estimate=cost(2 * height * count * BLOCK * half, height * (half + 512) * 2),
        name="term",
    )(order, *([turned[0]] * count), *([turned[1]] * count), delta, *adds, *after)


def settle_kernel(own_ref, *refs):
    refs[-1][...] = jnp.zeros_like(refs[-1])
    for n in range(2):
        one, two = refs[2 * n], refs[2 * n + 1]
        height = one.shape[0]
        value = own_ref[n * height : (n + 1) * height].astype(F32)
        value = value + one[...].astype(F32) + two[...].astype(F32)
        for k in range(2):
            refs[-SIDE - 1 + 2 * n + k][...] = value[k * BLOCK : (k + 1) * BLOCK].astype(BF)


def settle(own, tops, bottoms, after):
    height, half = own.shape
    slab = half // 2
    part = pl.BlockSpec((height // 2, slab), lambda i: (0, i))
    return pl.pallas_call(
        settle_kernel,
        out_shape=[jax.ShapeDtypeStruct((BLOCK, half), BF)] * SIDE + [MARKED],
        grid=(2,),
        in_specs=[pl.BlockSpec((height, slab), lambda i: (0, i))]
        + [part] * 4
        + [whole(MARK)] * len(after),
        out_specs=[pl.BlockSpec((BLOCK, slab), lambda i: (0, i))] * SIDE + [whole(MARK)],
        compiler_params=room(16),
        cost_estimate=cost(0, 8 * MIB),
        name="settle",
    )(own, *tops, *bottoms, *after)


def gather_kernel(*refs):
    value = refs[0][...].astype(F32)
    for ref in refs[1:SIDE]:
        value = value + ref[...].astype(F32)
    refs[-1][...] = value.astype(BF)


def gather(blocks, after):
    height, half = blocks[0].shape
    tile = pl.BlockSpec((height, half // 2), lambda i: (0, i))
    return pl.pallas_call(
        gather_kernel,
        out_shape=jax.ShapeDtypeStruct((height, half), BF),
        grid=(2,),
        in_specs=[tile] * SIDE + [whole(MARK)],
        out_specs=tile,
        compiler_params=room(12),
        cost_estimate=cost(0, 4 * MIB),
        name="gather",
    )(*blocks, after)


def back_kernel(order_ref, own_rows_ref, other_rows_ref, *refs):
    weights, (own_ref, other_ref, mark_ref, held, sems) = refs[: SIDE + 1], refs[-5:]
    mark_ref[...] = jnp.zeros_like(mark_ref)
    copies, at = [], 0
    for n, weight in enumerate(weights):
        height = weight.shape[0]
        copies.append(
            pltpu.make_async_copy(weight, held.at[pl.ds(at, height), :], sems.at[n])
        )
        copies[-1].start()
        at += height
    at = 0
    rows = own_ref.shape[0]
    left = jnp.concatenate([own_rows_ref[...], other_rows_ref[...]], axis=0)
    for n, weight in enumerate(weights):
        height = weight.shape[0]
        copies[n].wait()
        value = dot(left, held[at : at + height, :], NT)
        for k in range(height // BLOCK):
            place = columns(order_ref, at // BLOCK + k)
            piece = value[:, k * BLOCK : (k + 1) * BLOCK]
            own_ref[:, place] = piece[:rows]
            other_ref[:, place] = piece[rows:].astype(BF)
        at += height


def back(order, own, other, height, parts, after):
    half = own[0].shape[1]
    depth = sum(part.shape[0] for part in parts)
    return pl.pallas_call(
        back_kernel,
        out_shape=(
            jax.ShapeDtypeStruct((height, depth), F32),
            jax.ShapeDtypeStruct((height, depth), BF),
            MARKED,
        ),
        grid=(1,),
        in_specs=[SCALARS]
        + [pl.BlockSpec((height, half), lambda i, n=n: (n, 0)) for _, n in (own, other)]
        + [ANYWHERE] * len(parts)
        + [whole(MARK)] * len(after),
        out_specs=(whole((height, depth)), whole((height, depth)), whole(MARK)),
        scratch_shapes=[
            pltpu.VMEM((depth, half), BF),
            pltpu.SemaphoreType.DMA((len(parts),)),
        ],
        compiler_params=room(28),
        cost_estimate=cost(4 * height * depth * half, 14 * MIB),
        name="back",
    )(order, own[0], other[0], *parts, *after)


def combine_kernel(own_ref, got_ref, out_ref, mark_ref):
    mark_ref[...] = jnp.zeros_like(mark_ref)
    out_ref[...] = (own_ref[...] + got_ref[...].astype(F32)).astype(BF)


def combine(own, got):
    height, depth = own.shape
    tile = pl.BlockSpec((height, depth // 4), lambda i: (0, i))
    return pl.pallas_call(
        combine_kernel,
        out_shape=(jax.ShapeDtypeStruct(own.shape, BF), MARKED),
        grid=(4,),
        in_specs=[tile, tile],
        out_specs=(tile, whole(MARK)),
        compiler_params=room(12),
        cost_estimate=cost(0, 8 * height * depth),
        name="combine",
    )(own, got)


def lay_kernel(core_ref, own_ref, got_ref, out_ref, mark_ref):
    i = pl.program_id(0)
    mark_ref[...] = jnp.zeros_like(mark_ref)

    @pl.when(i < 2)
    def _():
        out_ref[...] = own_ref[...]

    @pl.when(i >= 2)
    def _():
        out_ref[...] = got_ref[...]


def lay(core, delta, got):
    height, half = got.shape
    quarter = half // 2
    return pl.pallas_call(
        lay_kernel,
        out_shape=(jax.ShapeDtypeStruct((height, 4 * quarter), BF), MARKED),
        grid_spec=pltpu.PrefetchScalarGridSpec(
            num_scalar_prefetch=1,
            grid=(4,),
            in_specs=[
                pl.BlockSpec((height, quarter), lambda i, core: (0, jnp.minimum(i, 1))),
                pl.BlockSpec((height, quarter), lambda i, core: (0, jnp.maximum(i - 2, 0))),
            ],
            out_specs=(pl.BlockSpec(
                (height, quarter),
                lambda i, core: (0, jnp.where(i < 2, 2 * core[0], 2 * (1 - core[0]) - 2) + i),
            ), whole(MARK)),
        ),
        compiler_params=room(12),
        cost_estimate=cost(0, 16 * height * quarter),
        name="lay",
    )(core, delta, got)


def body(query_attn, query_resid, passage_attn, passage_resid, out_weight, hard_lists, positive):
    z = lax.axis_index("dp")
    f = lax.axis_index("fsdp")
    c, x, y = f % CORES, (f // CORES) % SIDE, f // (SIDE * CORES)
    first = c == 0
    width = query_resid.shape[1]
    half = width // 2
    own_rows = passage_attn.shape[0]
    blocks = own_rows // BLOCK

    core = c.astype(jnp.int32).reshape(1)

    got = swap(other_halves(core, [out_weight, query_resid]))
    shard = chip_shard(core, out_weight, got)
    near = [shard, first_up(shard), first_down(shard), first_across(shard)]
    hops = jnp.array(HOPS, jnp.int32)
    ys, xs = (y + hops) % SIDE, (x + hops) % SIDE
    order = jnp.where(
        first, ys[:, None] * SIDE + xs[None, :], ys[None, :] * SIDE + xs[:, None]
    )
    order = order.reshape(-1).astype(jnp.int32)

    leading = lead(core, query_attn, query_resid)
    near_up, near_down = z_up(leading), z_down(leading)
    resid = pair_rows(core, query_resid, got)
    numbers = jnp.concatenate([hard_lists.reshape(-1), positive])
    other_numbers = swap(numbers)
    to_up, to_down, three = pack(query_attn, near_up, near_down, resid)
    from_up, from_down = z_up(to_up), z_down(to_down)
    weight = stack(near)
    parts = [weight, second_up(weight), second_down(weight)]
    pieces = [passage_attn, three, swap(passage_attn), swap(three)]
    main = own_rows + 3 * BLOCK
    places = [
        (0, 0, own_rows),
        (0, own_rows, 3 * BLOCK),
        (0, main, own_rows),
        (0, main + own_rows, 3 * BLOCK),
    ]
    span = own_rows + BLOCK
    other_resid = swap(other_half(core, passage_resid))
    resid_pieces = [passage_resid, resid, other_resid, resid]
    resid_places = [
        (None, 0, own_rows),
        (0, own_rows, BLOCK),
        (0, span, own_rows),
        (BLOCK, span + own_rows, BLOCK),
    ]
    total, rows, turned, mark = begin(
        order, core, weight, pieces, places, resid_pieces, resid_places
    )
    on_up, on_down = halves(parts[1], parts[2], [mark])
    parts += [second_up(on_up), second_down(on_down)]
    resid_up, resid_down, attn_far = repack(near_up, from_up, from_down, other_numbers)
    far_up, far_down = z_up(resid_up), z_down(resid_down)
    late = [attn_far, swap(attn_far)]

    total, lefts, turned_far = contract(order, total, rows, late, parts[:3])
    turned = (turned, turned_far)
    part = BLOCK // 2
    pieces = [near_up, near_down, from_up, from_down, far_up, far_down]
    places = [(BLOCK if n < 2 else part, n * BLOCK, BLOCK) for n in range(4)]
    places += [(0, n * BLOCK, BLOCK) for n in (4, 5)]
    low, raw, squares = mix(total, lefts, parts[3:], pieces, places, own_rows)
    squares = squares[0]
    raw = raw.reshape(CORES, SIDE, BLOCK, own_rows)

    squares = squares + jnp.concatenate(
        [squares_in for squares_in in (lambda v: (
            v[main : 2 * main], v[:main], v[2 * main + BLOCK :], v[2 * main : 2 * main + BLOCK]
        ))(swap(squares))]
    )
    squares = jnp.concatenate(
        [squares[: CORES * main].reshape(CORES, main), squares[CORES * main :].reshape(CORES, BLOCK)],
        axis=1,
    )
    squares_p = squares[:, :own_rows]
    squares_q = squares[:, own_rows:].reshape(CORES, SIDE, BLOCK)
    raw = raw + swap(raw)[::-1]
    factor_p = lax.rsqrt(squares_p + epsilon)
    factor_q = lax.rsqrt(squares_q + epsilon)

    listed = hard_lists.size
    lists = jnp.stack([numbers[:listed], other_numbers[:listed]]).reshape(CORES, SIDE, -1)
    ks = jnp.arange(SIDE, dtype=jnp.int32)
    source = (z + hops) % SIDE
    asked = jnp.take(lists, source, axis=1)
    ids = z * blocks + jnp.arange(blocks, dtype=jnp.int32)
    wanted = jnp.any(asked[:, :, :, None] == ids, axis=2)
    wanted = wanted | (ks == 0)[None, :, None]
    wanted = jnp.repeat(wanted, BLOCK, axis=2)[:, :, None, :]
    hits = jnp.stack([numbers[listed:], other_numbers[listed:]])
    target = (jnp.arange(own_rows, dtype=jnp.int32) == hits[:, :, None])[:, None]
    target = (target & (ks == 0)[None, :, None, None]).astype(F32)

    scores = sharpness * raw * factor_q[..., None] * factor_p[:, None, None, :]
    scores = jnp.where(wanted, scores, -1e30)
    highest = jnp.max(scores, axis=3)
    totals = jnp.sum(jnp.exp(scores - highest[..., None]), axis=3)
    stats = jnp.stack([highest, totals])
    all_stats = [stats]
    for k in range(1, SIDE):
        got = z_to[-HOPS[k] % SIDE](stats)
        picks = [[h % SIDE for h in HOPS].index((h - HOPS[k]) % SIDE) for h in HOPS]
        all_stats.append(jnp.concatenate([got[:, :, i : i + 1] for i in picks], axis=2))
    top = all_stats[0][0]
    for v in all_stats[1:]:
        top = jnp.maximum(top, v[0])
    log_total = top + jnp.log(sum(v[1] * jnp.exp(v[0] - top) for v in all_stats))
    query_loss = log_total[0, 0] - jnp.sum(scores[0, 0] * target[0, 0], axis=1)

    scale = sharpness / (BLOCK * DEVICES)
    grad = scale * (jnp.exp(scores - log_total[..., None]) - target)
    weighted = grad * scores * (1.0 / sharpness)
    inner_q = jnp.sum(weighted, axis=3)
    inner_p = jnp.sum(weighted, axis=(1, 2))
    grad_q = (grad * factor_p[:, None, None, :]).astype(BF).reshape(CORES, -1, own_rows)
    grad_p = (grad * factor_q[..., None]).astype(BF).reshape(CORES, -1, own_rows)
    factors = jnp.concatenate([factor_p, factor_q.reshape(CORES, -1)], axis=1)
    inners = jnp.concatenate([inner_p, inner_q.reshape(CORES, -1)], axis=1)
    coef = jnp.stack([factors, factors * factors * inners], axis=1)
    delta = project(low, grad_q, grad_p, coef)

    def at(e, j):
        return (e * main + own_rows) // BLOCK + j

    def both(e, j, k):
        return at(e, j), at(e, k)

    end = CORES * main // BLOCK
    far_top, far_bottom, mark = term(order, turned, delta, ((12, 13), (14, 15)))
    up, down = second_up(far_top), second_down(far_bottom)
    far, _ = join(core, delta, [((end + e,) * 2,) for e in range(CORES)], after=[mark])
    far = z_with(far)
    up_bottom, down_top, mark = term(
        order, turned, delta, ((10, 11), (4, 5)), after=[mark]
    )
    got_bottom, got_top = second_up(up_bottom), second_down(down_top)
    blocks = own_rows // BLOCK
    kept = [(both(0, k, k),) for k in range(-blocks, 1)] + [(both(1, 0, 0),)]
    mine, kept_mark = join(core, delta, kept, after=[mark])
    theirs, mark = join(
        core, delta, [(both(1, k, k),) for k in range(-blocks, 0)], after=[kept_mark]
    )
    up_top, down_bottom, mark = term(
        order, turned, delta, ((8, 9), (6, 7)), [up, down], [mark]
    )
    passage_delta, lay_mark = lay(core, mine, swap(theirs))
    got_tops = [got_top, second_up(up_top)]
    got_bottoms = [got_bottom, second_down(down_bottom)]
    own_sum, mark = term(order, turned, delta, ((0, 1, 2, 3),), after=[mark])
    flow, mark = join(
        core, delta, [(both(e, 2, 1), (0, e)) for e in range(CORES)], [far], [mark]
    )
    counter, counter_mark = join(
        core, delta, [(both(e, 1, 2),) for e in range(CORES)], after=[mark]
    )
    z_got = [z_with(flow), z_against(counter)]
    *sums, mark = settle(own_sum, got_tops, got_bottoms, [mark, counter_mark, lay_mark])
    own_back, other_back, back_mark = back(
        order, (mine, 0), (theirs, 0), own_rows, parts, [mark]
    )
    summed, _ = join(
        core,
        mine,
        [((blocks + e,) * 2, (0, e), (1, e)) for e in range(CORES)],
        z_got,
        [back_mark],
    )
    got = [sums[0], first_down(sums[1]), first_up(sums[2]), first_across(sums[3])]
    part = gather(got, back_mark)
    part = part.reshape(CORES, SIDE, BLOCK // 8, half)

    def pick(v, index, axis):
        return lax.dynamic_index_in_dim(v, index, axis, keepdims=False)

    total = pick(part, z, 1).astype(F32)
    for k in (1, 3, 2):
        total = total + z_to[k](pick(part, (z + k) % SIDE, 1)).astype(F32)
    total = total.astype(BF)
    own, other = pick(total, c, 0), swap(pick(total, 1 - c, 0))
    total = jnp.where(
        first, jnp.concatenate([own, other], axis=1), jnp.concatenate([other, own], axis=1)
    )
    late_mark = total[: MARK[0], : MARK[1]].astype(F32)
    weight_grad = jnp.zeros((SIDE,) + total.shape, F32)
    for k in (0, 1, 3, 2):
        got = total if k == 0 else z_to[k](total)
        weight_grad = lax.dynamic_update_index_in_dim(
            weight_grad, got.astype(F32), (z - k) % SIDE, 0
        )
    weight_grad = weight_grad.reshape(out_weight.shape)

    passage_back, back_mark = combine(own_back, swap(other_back))
    own_back, other_back, _ = back(
        order, (summed, 0), (summed, 1), BLOCK, parts, [late_mark]
    )
    query_back, _ = combine(own_back, swap(other_back))
    query_delta, _ = lay(core, summed, swap(summed[BLOCK:]))
    return (query_loss, query_back, query_delta, passage_back, passage_delta, weight_grad)


def solution(mesh):
    rows = P(("dp", "fsdp"), None)
    return jax.shard_map(
        body,
        mesh=mesh,
        in_specs=(
            rows,
            rows,
            rows,
            rows,
            P("fsdp", None),
            P("fsdp", None, None),
            P(("dp", "fsdp")),
        ),
        out_specs=(P(("dp", "fsdp")), rows, rows, rows, rows, P("fsdp", None)),
        check_vma=False,
    )
```
